512 devices in a mesh: lib: 64 (over z, y), qry: 8 (over x, core).
Axes of the slice: x: 4, y: 4, z: 16, core: 2. Of those that a mesh axis runs over, the one named last changes fastest.
Arguments:
- queries: bfloat16 [32768, 1024], P(('lib', 'qry')), may hold values from -0.75 to 0.75
- owner: int32 [32768, 1], P(('lib', 'qry')), may hold values from 0 to 63; in each aligned block of 64 rows (0 to 63, 64 to 127, ...) at most 2 rows name the same one
- window_start: int32 [32768], P(('lib', 'qry')), may hold values from 0 to 16
- peak_bins: int32 [65536, 128], P(('lib', 'qry')), may hold values from 0 to 1023
- peak_int: bfloat16 [65536, 128], P(('lib', 'qry')), may hold values from 0.099609375 to 1
- block_shift: int32 [512], P(('lib', 'qry')), may hold values from -256 to 256
Outputs:
- block_scores: float32 [32768, 8], P(('lib', 'qry'))
The draws below stay inside these ranges and needn't reach their ends.
Inputs may be any that keep to these rules, and one draw needn't show every extreme that they name: Among the 64 queries of one device at most 2 have the same owner; in some devices one owner is named exactly 2 times.
All inputs are finite; a program needn't handle non-finite values.
Results may differ from the reference program's by a relative error of at most 0.00081.
Values may be sent and summed in bfloat16 or wider, within the bound.
A program may use at most 64 MiB of HBM per device.

```python
import math
import jax
import jax.numpy as jnp
import numpy as np
from jax import lax

B = 1024
P_SIZE = 128
CB = 128
BLK_DEV = 1
QRY_DEV = 64
BPS = 8
WIN = 8
CAP = 2
Q = 32768
LIBN = 65536
NBLK = 512
N_LIB = 64
N_QRY = 8


def plant(drawn, key, low, largest):
    dims = drawn.shape
    place = [jax.random.randint(jax.random.fold_in(key, axis), (), 0, dims[axis]) for axis in range(len(dims))]
    drawn = drawn.at[tuple(place)].set(low)
    longest = dims.index(max(dims))
    place[longest] = (place[longest] + 1) % dims[longest]
    return drawn.at[tuple(place)].set(largest)


def levels(rng, extent, cuts, smallest, top_value):
    gain = 1.0
    for position, parts in cuts:
        steps = jax.random.uniform(jax.random.fold_in(jax.random.fold_in(rng, 6), position), (parts,), jnp.float32, smallest / len(cuts), top_value / len(cuts))
        gain = gain * jnp.repeat(jnp.exp(steps), extent[position] // parts).reshape((-1,) + (1,) * (len(extent) - 1 - position))
    return gain


def deal_out(rng, own, number, rows, count, top, bound, lean):
    order = jax.random.permutation(rng, count)
    packed, usual = shares(count, rows * top, bound, lean, True), shares(count, rows * top, bound, lean, False)
    places = jnp.arange(count)

    def named(lengths, turn):
        used = int((lengths > 0).sum())
        fixed = max(1, used // 4)
        passed = fixed + (places - fixed + turn * (used - fixed)) % max(1, count - fixed)
        return jnp.zeros((count,), jnp.int32).at[order[jnp.where(places < fixed, places, passed)]].set(jnp.asarray(lengths, jnp.int32))

    lengths = jnp.where(number % 4 == 0, named(packed, number // 4), named(usual, number - number // 4 - 1))
    mixed = jax.random.permutation(jax.random.fold_in(own, 3), count)
    donor, sink = mixed[0:count // 2 * 2:2], mixed[1:count // 2 * 2:2]
    room = jnp.minimum(lengths[donor] - 1, bound - lengths[sink]) // 2
    room = jnp.where((donor == order[0]) | (sink == order[0]) | (lengths[sink] == 0), 0, jnp.maximum(room, 0))
    passed = jax.random.randint(jax.random.fold_in(own, 4), (count // 2,), 0, 1 << 20) % (room + 1)
    lengths = lengths.at[donor].add(-passed).at[sink].add(passed)
    members = jnp.searchsorted(jnp.cumsum(lengths), jnp.arange(rows * top), side="right").astype(jnp.int32)
    listing = members.reshape(top, rows).T
    listing = listing[jax.random.permutation(jax.random.fold_in(own, 1), rows)]
    turn = jax.random.randint(jax.random.fold_in(own, 2), (rows, 1), 0, top)
    return jnp.take_along_axis(listing, (jnp.arange(top)[None, :] + turn) % top, axis=1)


def shares(count, total, most, skew, full):
    loads = [(1 << 20) // math.isqrt(standing ** skew) + 1 for standing in range(1, count + 1)]
    largest = most if full else min(most, max(-(-total // count), total * loads[0] // sum(loads)))
    least = 1 if total - largest >= count - 1 else 0
    given, spare = [largest] + [least] * (count - 1), total - largest - least * (count - 1)
    while spare > 0:
        candidates = [i for i in range(1, count) if given[i] < largest] or [i for i in range(1, count) if given[i] < most]
        mass, remaining = sum([loads[i] for i in candidates]), spare
        for i in candidates:
            extra = min(most - given[i], max(1, remaining * loads[i] // mass), spare)
            given[i] = given[i] + extra
            spare = spare - extra
    return np.array(given)


def gaussian(own_key, dims, spread, most, pieces=(), kind=jnp.bfloat16):
    drawn = jax.random.normal(own_key, dims, jnp.float32) * spread
    if len(pieces) > 0:
        drawn = levels(own_key, dims, pieces, -0.22, 0.18) * drawn
    return jnp.clip(drawn, min=-most, max=most).astype(kind)


def setup_inputs(seed: int = 0) -> dict:
    key_of = jax.random.split(jax.random.key(seed), 7)
    queries = gaussian(key_of[0], (Q, B), 0.125, 0.75, ((0, 512),))
    owner_keys = jax.random.split(jax.random.fold_in(key_of[1], 1), Q // QRY_DEV)
    owner_turns = jax.random.permutation(jax.random.fold_in(key_of[1], 3), Q // QRY_DEV)
    owner = jax.vmap(lambda own, number: deal_out(jax.random.fold_in(key_of[1], 2), own, number, QRY_DEV, N_LIB, 1, CAP, 2))(owner_keys, owner_turns).reshape((Q, 1))
    window_start = plant(jax.random.randint(key_of[2], (Q,), 0, 2 * BPS + 1), jax.random.fold_in(key_of[2], 1), 0, 2 * BPS).astype(jnp.int32)
    peak_bins = plant(jax.random.randint(key_of[3], (LIBN, P_SIZE), 0, B), jax.random.fold_in(key_of[3], 1), 0, B - 1).astype(jnp.int32)
    peak_int = jnp.clip(jnp.exp(math.log(1.0) - 2.306499 * jax.random.uniform(key_of[4], (LIBN, P_SIZE), jnp.float32) ** levels(key_of[4], (LIBN, P_SIZE), ((0, 512),), -0.2, 0.2)), 0.099609375, 1.0).astype(jnp.bfloat16)
    block_shift = plant(jax.random.randint(key_of[5], (NBLK,), 0 - B // 4, B // 4 + 1), jax.random.fold_in(key_of[5], 1), 0 - B // 4, (B // 4 + 1) - 1).astype(jnp.int32)
    return dict(queries=queries, owner=owner, window_start=window_start, peak_bins=peak_bins, peak_int=peak_int, block_shift=block_shift)


def densify(bins, intensity, shift_rows):
    row_count = bins.shape[0]
    row_ids = jnp.broadcast_to(jnp.arange(row_count, dtype=jnp.int32)[:, None], bins.shape)
    weights = intensity.astype(jnp.float32)
    moved = bins + shift_rows[:, None]
    inside = (moved >= 0) & (moved < B)
    shifted_weights = jnp.where(inside, weights, jnp.zeros_like(weights))
    dense = jnp.zeros((row_count, B), jnp.float32).at[row_ids, bins].add(weights)
    dense = dense.at[row_ids, jnp.clip(moved, 0, B - 1)].add(shifted_weights)
    return dense.astype(jnp.bfloat16)


def reference(queries, owner, window_start, peak_bins, peak_int, block_shift):
    block_total = block_shift.shape[0]
    range_blocks = BLK_DEV * N_QRY
    bins_blocks = peak_bins.reshape(block_total, CB, P_SIZE)
    int_blocks = peak_int.reshape(block_total, CB, P_SIZE)

    def make_block(items):
        return densify(items[0], items[1], jnp.full((CB,), items[2], jnp.int32))

    dense = lax.map(make_block, (bins_blocks, int_blocks, block_shift))
    padding = jnp.zeros((range_blocks, CB, B), jnp.bfloat16)
    padded = jnp.concatenate([padding, dense, padding], axis=0)
    total_queries = queries.shape[0]
    limit = min(total_queries, (total_queries // QRY_DEV) * CAP)
    targets = owner[:, 0]

    def per_owner(collected, owner_id):
        nearby = lax.dynamic_slice_in_dim(padded, owner_id * range_blocks, 3 * range_blocks, 0)
        nearby = nearby.reshape(3 * range_blocks * CB, B)
        picked = jnp.nonzero(targets == owner_id, size=limit, fill_value=total_queries)[0].astype(jnp.int32)
        rows = queries[jnp.minimum(picked, total_queries - 1)]
        scores = lax.dot_general(rows, nearby, (((1,), (1,)), ((), ())), preferred_element_type=jnp.float32)
        best = scores.reshape(limit, 3 * range_blocks, CB).max(axis=2)
        collected = collected.at[picked].set(best, mode="drop")
        return collected, None

    start = jnp.zeros((total_queries, 3 * range_blocks), jnp.float32)
    collected, _ = lax.scan(per_owner, start, jnp.arange(N_LIB, dtype=jnp.int32))
    chosen = window_start[:, None] + jnp.arange(WIN, dtype=jnp.int32)[None, :]
    return jnp.take_along_axis(collected, chosen, axis=1)
```

```python
import functools

import jax
import jax.numpy as jnp
from jax import lax
from jax.experimental import pallas as pl
from jax.experimental.pallas import tpu as pltpu
from jax.sharding import PartitionSpec as P

MESH = pl.DeviceIdType.MESH
B = 1024
NZ, NY, NX = 16, 4, 4
NL = NZ * NY
ROWS = 64
CB = 128
LANES = 128
CHUNKS = B // LANES
GROUPS = 4
GSRC = NL // GROUPS
BF, F32, I32 = jnp.bfloat16, jnp.float32, jnp.int32


def iota(shape, axis):
    return lax.broadcasted_iota(I32, shape, axis)


def offset(index):
    k, dy = index // NY, index % NY
    dz = jnp.where(k % 2 == 1, (k + 1) // 2, lax.rem(NZ - k // 2, NZ))
    return dz, dy


def ahead(l, index):
    dz, dy = offset(index)
    return lax.rem(l // NY + dz, NZ) * NY + lax.rem(l % NY + dy, NY)


def behind(l, index):
    dz, dy = offset(index)
    return lax.rem(l // NY + NZ - dz, NZ) * NY + lax.rem(l % NY + NY - dy, NY)


def place_of(owner, l):
    dz = (owner // NY - l // NY + NZ) % NZ
    dy = (owner % NY - l % NY + NY) % NY
    k = jnp.where(dz == 0, 0, jnp.where(dz <= NZ // 2, 2 * dz - 1, 2 * (NZ - dz)))
    return k * NY + dy


def to_row(column):
    n = column.shape[0]
    return jnp.sum(jnp.where(iota((n, n), 0) == iota((n, n), 1), column, 0.0), axis=0, keepdims=True)


def to_column(row):
    n = row.shape[1]
    return jnp.sum(jnp.where(iota((n, n), 0) == iota((n, n), 1), row, 0.0), axis=1, keepdims=True)


def kernel(
    q_hbm, owner_hbm, window_hbm, bins_hbm, int_hbm, shift_hbm,
    out_ref,
    q_ref, owner_ref, window_ref, bins_ref, int_ref, shift_ref, load_sem,
    tall, outgoing, qbuf, qmat, hi_ref, lo_ref, w_ref, dense, maxima, back, xback, ret_src, ret_dst,
    raw_send, raw_recv, mate_send, mate_recv, a2a_send, a2a_recv, fwd_send, fwd_recv, xb_send, xb_recv,
    ret_send, ret_recv,
):
    l, q = lax.axis_index("lib"), lax.axis_index("qry")
    x, core = q // 2, q % 2
    mate = (l, x * 2 + 1 - core)

    def beside(dx):
        return (l, lax.rem(x + dx, NX) * 2 + core)

    loads = [
        pltpu.make_async_copy(src, dst, load_sem.at[i])
        for i, (src, dst) in enumerate(
            (
                (owner_hbm, owner_ref),
                (q_hbm, q_ref),
                (window_hbm, window_ref),
                (shift_hbm, shift_ref.at[0]),
                (bins_hbm, bins_ref.at[0]),
                (int_hbm, int_ref.at[0]),
            )
        )
    ]
    for load in loads:
        load.start()

    barrier = pltpu.get_barrier_semaphore()

    def greet(i, carry):
        pl.semaphore_signal(barrier, inc=1, device_id=(ahead(l, i), q), device_id_type=MESH)
        return carry

    lax.fori_loop(1, NL, greet, 0)
    for dx in range(1, NX):
        pl.semaphore_signal(barrier, inc=1, device_id=beside(dx), device_id_type=MESH)
    pl.semaphore_signal(barrier, inc=1, device_id=mate, device_id_type=MESH)
    for load in loads:
        load.wait()

    owner = owner_ref[...]
    owner_col = owner.astype(F32)
    owner_row = to_row(owner_col)
    square = (ROWS, ROWS)
    earlier = (owner_col == owner_row) & (iota(square, 1) < iota(square, 0))
    turn = jnp.sum(jnp.where(earlier, 1.0, 0.0), axis=1, keepdims=True)
    place = place_of(owner, l).astype(F32)
    slot_row = to_row(place * 2.0 + turn)
    pick = jnp.where(iota((2 * NL, ROWS), 0).astype(F32) == slot_row, 1.0, 0.0).astype(BF)
    rows = jnp.dot(pick, q_ref[...], preferred_element_type=F32)
    for j in range(CHUNKS):
        tall[pl.ds(j, 2 * NL, stride=CHUNKS), :] = rows[:, j * LANES : (j + 1) * LANES]
    outgoing[...] = tall[...].astype(BF).reshape(NL, 16, LANES)
    qbuf[0, 0] = outgoing[0]

    def densify(r):
        bins, weights = bins_ref[r], int_ref[r].astype(F32)
        moved = bins + shift_ref[r, 0:1, :]
        hi_ref[:, 0:LANES] = (bins >> 7).astype(F32)
        hi_ref[:, LANES:] = (moved >> 7).astype(F32)
        lo_ref[:, 0:LANES] = (bins & 127).astype(F32)
        lo_ref[:, LANES:] = (moved & 127).astype(F32)
        w_ref[:, 0:LANES] = weights
        w_ref[:, LANES:] = weights
        hi_ids = iota((CHUNKS, 2 * LANES), 0).astype(F32)
        lo_ids = iota((LANES, 2 * LANES), 0).astype(F32)

        def eight(i, carry):
            at = pl.ds(pl.multiple_of(i * 8, 8), 8)
            his, los, ws = hi_ref[at, :], lo_ref[at, :], w_ref[at, :]
            for c in range(8):
                a = jnp.where(hi_ids == his[c : c + 1, :], ws[c : c + 1, :], 0.0).astype(BF)
                b = jnp.where(lo_ids == los[c : c + 1, :], 1.0, 0.0).astype(BF)
                d = lax.dot_general(a, b, (((1,), (1,)), ((), ())), preferred_element_type=F32)
                tall[pl.ds(pl.multiple_of(i * 64, 64) + c * 8, 8), :] = d
            return carry

        lax.fori_loop(0, CB // 8, eight, 0)
        for j in range(CHUNKS):
            dense[r, :, j * LANES : (j + 1) * LANES] = tall[pl.ds(j, CB, stride=CHUNKS), :].astype(BF)

    def to_mate(r):
        return pltpu.make_async_remote_copy(
            src_ref=dense.at[r], dst_ref=dense.at[3 + r], send_sem=mate_send.at[r], recv_sem=mate_recv.at[r],
            device_id=mate, device_id_type=MESH,
        )

    densify(0)
    pl.semaphore_wait(barrier, NL - 1 + NX - 1 + 1)

    raw = []
    for slot, to in ((1, lax.rem(l + 1, NL)), (2, lax.rem(l + NL - 1, NL))):
        for i, ref in enumerate((bins_ref, int_ref, shift_ref)):
            raw.append(
                pltpu.make_async_remote_copy(
                    src_ref=ref.at[0], dst_ref=ref.at[slot], send_sem=raw_send.at[slot - 1, i],
                    recv_sem=raw_recv.at[slot - 1, i], device_id=(to, q), device_id_type=MESH,
                )
            )
    for copy in raw:
        copy.start()

    def deal(i, carry):
        pltpu.make_async_remote_copy(
            src_ref=outgoing.at[i], dst_ref=qbuf.at[0, i], send_sem=a2a_send, recv_sem=a2a_recv.at[i // GSRC],
            device_id=(ahead(l, i), q), device_id_type=MESH,
        ).start()
        return carry

    lax.fori_loop(1, NL, deal, 0)
    mates = [to_mate(0)]
    mates[0].start()
    for slot in (1, 2):
        for i in range(3):
            raw[(slot - 1) * 3 + i].wait_recv()
        densify(slot)
        mates.append(to_mate(slot))
        mates[slot].start()

    def group(g):
        return pl.ds(g * GSRC, GSRC)

    forwards = []

    def forward(g):
        arrived = qbuf.at[0, pl.ds(1, GSRC - 1)] if g == 0 else qbuf.at[0, group(g)]
        pltpu.make_async_copy(arrived, arrived, a2a_recv.at[g]).wait()
        copies = [
            pltpu.make_async_remote_copy(
                src_ref=qbuf.at[0, group(g)], dst_ref=qbuf.at[dx, group(g)], send_sem=fwd_send.at[g, dx - 1],
                recv_sem=fwd_recv.at[g, dx - 1], device_id=beside(dx), device_id_type=MESH,
            )
            for dx in range(1, NX)
        ]
        for copy in copies:
            copy.start()
        forwards.append(copies)

    def score(g):
        for copy in forwards[g]:
            copy.wait_recv()
        if g == 0:
            for copy in mates:
                copy.wait_recv()
        for dx in range(NX):
            part = qbuf[dx, group(g)].reshape(GSRC * 16, LANES)
            tall[pl.ds(dx * GSRC * 16, GSRC * 16), :] = part.astype(F32)
        for j in range(CHUNKS):
            for dx in range(NX):
                for s in range(2):
                    qmat[pl.ds((dx * 2 + s) * GSRC, GSRC), j * LANES : (j + 1) * LANES] = tall[
                        pl.ds(dx * GSRC * 16 + s * 8 + j, GSRC, stride=16), :
                    ].astype(BF)

        def block(b, carry):
            scores = lax.dot_general(
                dense[b], qmat[...], (((1,), (1,)), ((), ())), preferred_element_type=F32
            )
            top = jnp.max(scores, axis=0, keepdims=True)
            return jnp.where(iota((8, LANES), 0) == b, top, carry)

        maxima[g] = lax.fori_loop(0, 6, block, jnp.zeros((8, LANES), F32))

    forward(0)
    forward(1)
    score(0)
    forward(2)
    score(1)
    forward(3)
    score(2)
    score(3)

    lane = iota((8, LANES), 1)
    for dx in range(NX):
        total = jnp.zeros((8, LANES), F32)
        for g in range(GROUPS):
            turned = pltpu.roll(maxima[g], ((g - dx) * 32) % LANES, 1) if g != dx else maxima[g]
            total = jnp.where(lane // 32 == g, turned, total)
        if dx == 0:
            xback[0] = total
        else:
            back[dx] = total
    xbacks = [
        pltpu.make_async_remote_copy(
            src_ref=back.at[dx], dst_ref=xback.at[dx], send_sem=xb_send.at[dx - 1], recv_sem=xb_recv.at[dx - 1],
            device_id=beside(NX - dx), device_id_type=MESH,
        )
        for dx in range(1, NX)
    ]
    for copy in xbacks:
        copy.start()
    for copy in xbacks:
        copy.wait_recv()
    wide = jnp.concatenate([xback[...].reshape(NX * 8, LANES), jnp.zeros((LANES - NX * 8, LANES), F32)], axis=0)
    slots = wide.T
    for g in range(GROUPS):
        first = slots[g * 32 : g * 32 + 16, :]
        second = slots[g * 32 + 16 : g * 32 + 32, :]
        ret_src[group(g), 0, :] = first + pltpu.roll(second, 64, 1)
    ret_dst[0] = ret_src[0]

    def give_back(i, carry):
        pltpu.make_async_remote_copy(
            src_ref=ret_src.at[i], dst_ref=ret_dst.at[i], send_sem=ret_send, recv_sem=ret_recv,
            device_id=(behind(l, i), q), device_id_type=MESH,
        ).start()
        return carry

    lax.fori_loop(1, NL, give_back, 0)

    window = to_column(window_ref[...].astype(F32)).astype(I32)
    lanes = []
    for k in range(8):
        block_id = window + k
        r, col = block_id // 8, block_id % 8
        dx = (col // 2 - x + NX) % NX
        slot = jnp.where(r == 0, 1, jnp.where(r == 1, 0, 2))
        row = jnp.where(col % 2 == core, slot, 3 + slot)
        out_of_range = ((owner == 0) & (r == 0)) | ((owner == NL - 1) & (r == 2))
        target = dx * 8 + row + turn.astype(I32) * 64
        lanes.append(jnp.where(out_of_range, -1, target))
    take = jnp.where(iota((ROWS, NL), 1) == place.astype(I32), 1.0, 0.0)

    others = pl.ds(1, NL - 1)
    pltpu.make_async_copy(ret_dst.at[others], ret_dst.at[others], ret_recv).wait()
    mine = jnp.dot(take, ret_dst[:, 0, :], precision=lax.Precision.HIGHEST, preferred_element_type=F32)
    result = jnp.zeros((ROWS, 8), F32)
    for k in range(8):
        value = jnp.sum(jnp.where(iota((ROWS, LANES), 1) == lanes[k], mine, 0.0), axis=1, keepdims=True)
        result = jnp.where(iota((ROWS, 8), 1) == k, value, result)
    out_ref[...] = result

    for copy in raw:
        copy.wait_send()
    for copy in mates:
        copy.wait_send()
    for copies in forwards:
        for copy in copies:
            copy.wait_send()
    for copy in xbacks:
        copy.wait_send()
    pltpu.make_async_copy(outgoing.at[others], outgoing.at[others], a2a_send).wait()
    pltpu.make_async_copy(ret_src.at[others], ret_src.at[others], ret_send).wait()


def per_device(queries, owner, window_start, peak_bins, peak_int, block_shift):
    window_row = window_start.reshape(1, ROWS)
    shift = jnp.broadcast_to(block_shift.reshape(1, 1), (8, LANES))
    dma = pltpu.SemaphoreType.DMA
    anywhere = pl.BlockSpec(memory_space=pl.ANY)
    return pl.pallas_call(
        kernel,
        out_shape=jax.ShapeDtypeStruct((ROWS, 8), F32),
        in_specs=[anywhere] * 6,
        out_specs=pl.BlockSpec(memory_space=pltpu.VMEM),
        scratch_shapes=[
            pltpu.VMEM((ROWS, B), BF),
            pltpu.VMEM((ROWS, 1), I32),
            pltpu.VMEM((1, ROWS), I32),
            pltpu.VMEM((3, CB, LANES), I32),
            pltpu.VMEM((3, CB, LANES), BF),
            pltpu.VMEM((3, 8, LANES), I32),
            dma((6,)),
            pltpu.VMEM((1024, LANES), F32),
            pltpu.VMEM((NL, 16, LANES), BF),
            pltpu.VMEM((NX, NL, 16, LANES), BF),
            pltpu.VMEM((LANES, B), BF),
            pltpu.VMEM((CB, 2 * LANES), F32),
            pltpu.VMEM((CB, 2 * LANES), F32),
            pltpu.VMEM((CB, 2 * LANES), F32),
            pltpu.VMEM((6, CB, B), BF),
            pltpu.VMEM((GROUPS, 8, LANES), F32),
            pltpu.VMEM((NX, 8, LANES), F32),
            pltpu.VMEM((NX, 8, LANES), F32),
            pltpu.VMEM((NL, 1, LANES), F32),
            pltpu.VMEM((NL, 1, LANES), F32),
            dma((2, 3)), dma((2, 3)),
            dma((3,)), dma((3,)),
            dma, dma((GROUPS,)),
            dma((GROUPS, NX - 1)), dma((GROUPS, NX - 1)),
            dma((NX - 1,)), dma((NX - 1,)),
            dma, dma,
        ],
        compiler_params=pltpu.CompilerParams(
            collective_id=0, has_side_effects=True, vmem_limit_bytes=24 * 1024 * 1024
        ),
    )(queries, owner, window_row, peak_bins, peak_int, shift)


def solution(mesh):
    both = ("lib", "qry")
    placed = (P(both, None), P(both, None), P(both), P(both, None), P(both, None), P(both))
    return jax.shard_map(
        per_device, mesh=mesh, in_specs=placed, out_specs=P(both, None), check_vma=False
    )
```

```python
import functools

import jax
import jax.numpy as jnp
from jax import lax
from jax.experimental import pallas as pl
from jax.experimental.pallas import tpu as pltpu
from jax.sharding import PartitionSpec as P

MESH = pl.DeviceIdType.MESH
B = 1024
NZ, NY, NX = 16, 4, 4
NL = NZ * NY
ROWS = 64
CB = 128
LANES = 128
CHUNKS = B // LANES
GROUPS = 4
GSRC = NL // GROUPS
PIECES = 8
PSRC = NL // PIECES
HIS, LOS = 16, 64
UNROLL = 32
BF, F32, I32 = jnp.bfloat16, jnp.float32, jnp.int32


def iota(shape, axis):
    return lax.broadcasted_iota(I32, shape, axis)


def offset(index):
    k, dy = index // NY, index % NY
    dz = jnp.where(k % 2 == 1, (k + 1) // 2, lax.rem(NZ - k // 2, NZ))
    return dz, dy


def ahead(l, index):
    dz, dy = offset(index)
    return lax.rem(l // NY + dz, NZ) * NY + lax.rem(l % NY + dy, NY)


def behind(l, index):
    dz, dy = offset(index)
    return lax.rem(l // NY + NZ - dz, NZ) * NY + lax.rem(l % NY + NY - dy, NY)


def place_of(owner, l):
    dz = (owner // NY - l // NY + NZ) % NZ
    dy = (owner % NY - l % NY + NY) % NY
    k = jnp.where(dz == 0, 0, jnp.where(dz <= NZ // 2, 2 * dz - 1, 2 * (NZ - dz)))
    return k * NY + dy


def to_row(column):
    n = column.shape[0]
    return jnp.sum(jnp.where(iota((n, n), 0) == iota((n, n), 1), column, 0.0), axis=0, keepdims=True)


def to_column(row):
    n = row.shape[1]
    return jnp.sum(jnp.where(iota((n, n), 0) == iota((n, n), 1), row, 0.0), axis=1, keepdims=True)


def kernel(
    q_hbm, owner_hbm, window_hbm, bins_hbm, int_hbm, shift_smem,
    out_ref,
    q_ref, owner_ref, window_ref, peaks_ref, bins_ref, int_ref, shift_ref, load_sem,
    tall, outgoing, qbuf, qmat, hi_ref, lo_ref, w_ref, dense, maxima, back, xback, ret_src, ret_dst,
    raw_send, raw_recv, mate_send, mate_recv, a2a_send, a2a_recv, fwd_send, fwd_recv, xb_send, xb_recv,
    ret_send, ret_recv,
):
    l, q = lax.axis_index("lib"), lax.axis_index("qry")
    x, core = q // 2, q % 2
    mate = (l, x * 2 + 1 - core)

    def beside(dx):
        return (l, lax.rem(x + dx, NX) * 2 + core)

    loads = [
        pltpu.make_async_copy(src, dst, load_sem.at[i])
        for i, (src, dst) in enumerate(
            (
                (owner_hbm, owner_ref),
                (q_hbm, q_ref),
                (window_hbm, window_ref),
                (bins_hbm, peaks_ref),
                (int_hbm, int_ref.at[0]),
            )
        )
    ]
    for load in loads:
        load.start()

    barrier = pltpu.get_barrier_semaphore()

    def greet(i, carry):
        pl.semaphore_signal(barrier, inc=1, device_id=(ahead(l, i), q), device_id_type=MESH)
        return carry

    lax.fori_loop(1, NL, greet, 0)
    for dx in range(1, NX):
        pl.semaphore_signal(barrier, inc=1, device_id=beside(dx), device_id_type=MESH)
    pl.semaphore_signal(barrier, inc=1, device_id=mate, device_id_type=MESH)
    for load in loads[:2]:
        load.wait()

    owner_row = owner_ref[...].astype(F32)
    owner_col = to_column(owner_row)
    owner = owner_col.astype(I32)
    square = (ROWS, ROWS)
    earlier = (owner_col == owner_row) & (iota(square, 1) < iota(square, 0))
    turn = jnp.sum(jnp.where(earlier, 1.0, 0.0), axis=1, keepdims=True)
    place = place_of(owner, l).astype(F32)
    slot_row = to_row(place * 2.0 + turn)
    pick = jnp.where(iota((2 * NL, ROWS), 0).astype(F32) == slot_row, 1.0, 0.0).astype(BF)
    rows = jnp.dot(pick, q_ref[...], preferred_element_type=F32)
    for j in range(CHUNKS):
        tall[pl.ds(j, 2 * NL, stride=CHUNKS), :] = rows[:, j * LANES : (j + 1) * LANES]
    outgoing[...] = tall[...].astype(BF).reshape(NL, 16, LANES)
    qbuf[0, 0] = outgoing[0]

    def densify(r):
        bins, weights = bins_ref[r].astype(I32), int_ref[r].astype(F32)
        moved = bins + shift_ref[r, 0:1, :]
        hi_ref[:, 0:LANES] = (bins >> 6).astype(F32)
        hi_ref[:, LANES:] = (moved >> 6).astype(F32)
        lo_ref[:, 0:LANES] = (bins & (LOS - 1)).astype(F32)
        lo_ref[:, LANES:] = (moved & (LOS - 1)).astype(F32)
        w_ref[:, 0:LANES] = weights
        w_ref[:, LANES:] = weights
        hi_ids = iota((HIS, 2 * LANES), 0).astype(F32)
        lo_ids = iota((LOS, 2 * LANES), 0).astype(F32)
        left = iota((HIS, LANES), 1) < LOS

        def some(i, carry):
            at = pl.ds(pl.multiple_of(i * UNROLL, UNROLL), UNROLL)
            his, los, ws = hi_ref[at, :], lo_ref[at, :], w_ref[at, :]
            for c in range(0, UNROLL, 2):
                a = [jnp.where(hi_ids == his[e : e + 1, :], ws[e : e + 1, :], 0.0).astype(BF) for e in (c, c + 1)]
                b = [jnp.where(lo_ids == los[e : e + 1, :], 1.0, 0.0).astype(BF) for e in (c, c + 1)]
                d = lax.dot_general(
                    jnp.concatenate(a, 0), jnp.concatenate(b, 0), (((1,), (1,)), ((), ())),
                    preferred_element_type=F32,
                )
                row = pl.multiple_of(i * (UNROLL * 8), UNROLL * 8) + c * 8
                tall[pl.ds(row, HIS), :] = jnp.where(left, d[:HIS], d[HIS:])
            return carry

        lax.fori_loop(0, CB // UNROLL, some, 0)
        half = iota((CB // 2, LANES), 1) < LOS
        for j in range(CHUNKS):
            e = tall[pl.ds(2 * j, CB // 2, stride=HIS), :]
            f = tall[pl.ds(2 * j + 1, CB // 2, stride=HIS), :]
            at = slice(j * LANES, (j + 1) * LANES)
            dense[r, 0 : CB // 2, at] = jnp.where(half, e, pltpu.roll(f, LOS, 1)).astype(BF)
            dense[r, CB // 2 :, at] = jnp.where(half, pltpu.roll(e, LOS, 1), f).astype(BF)

    def to_mate(r):
        return pltpu.make_async_remote_copy(
            src_ref=dense.at[r], dst_ref=dense.at[3 + r], send_sem=mate_send.at[r], recv_sem=mate_recv.at[r],
            device_id=mate, device_id_type=MESH,
        )

    for load in loads[2:]:
        load.wait()
    bins_ref[0] = peaks_ref[...].astype(jnp.int16)
    shift_ref[0] = jnp.full((8, LANES), shift_smem[0], I32)
    densify(0)
    pl.semaphore_wait(barrier, NL - 1 + NX - 1 + 1)

    raw = []
    for slot, to in ((1, lax.rem(l + 1, NL)), (2, lax.rem(l + NL - 1, NL))):
        for i, ref in enumerate((bins_ref, int_ref, shift_ref)):
            raw.append(
                pltpu.make_async_remote_copy(
                    src_ref=ref.at[0], dst_ref=ref.at[slot], send_sem=raw_send.at[slot - 1, i],
                    recv_sem=raw_recv.at[slot - 1, i], device_id=(to, q), device_id_type=MESH,
                )
            )
    for copy in raw:
        copy.start()

    def deal(i, carry):
        pltpu.make_async_remote_copy(
            src_ref=outgoing.at[i], dst_ref=qbuf.at[0, i], send_sem=a2a_send, recv_sem=a2a_recv.at[i // PSRC],
            device_id=(ahead(l, i), q), device_id_type=MESH,
        ).start()
        return carry

    lax.fori_loop(1, NL, deal, 0)
    mates = [to_mate(0)]
    mates[0].start()
    for slot in (1, 2):
        for i in range(3):
            raw[(slot - 1) * 3 + i].wait_recv()
        densify(slot)
        mates.append(to_mate(slot))
        mates[slot].start()

    forwards = []

    def forward(p):
        piece = pl.ds(p * PSRC, PSRC)
        arrived = qbuf.at[0, pl.ds(1, PSRC - 1)] if p == 0 else qbuf.at[0, piece]
        pltpu.make_async_copy(arrived, arrived, a2a_recv.at[p]).wait()
        copies = [
            pltpu.make_async_remote_copy(
                src_ref=qbuf.at[0, piece], dst_ref=qbuf.at[dx, piece], send_sem=fwd_send.at[p, dx - 1],
                recv_sem=fwd_recv.at[p, dx - 1], device_id=beside(dx), device_id_type=MESH,
            )
            for dx in range(1, NX)
        ]
        for copy in copies:
            copy.start()
        forwards.append(copies)

    def group(g):
        return pl.ds(g * GSRC, GSRC)

    def score(g):
        for copies in forwards[2 * g : 2 * g + 2]:
            for copy in copies:
                copy.wait_recv()
        if g == 0:
            for copy in mates:
                copy.wait_recv()
        for dx in range(NX):
            part = qbuf[dx, group(g)].reshape(GSRC * 16, LANES)
            tall[pl.ds(dx * GSRC * 16, GSRC * 16), :] = part.astype(F32)
        for j in range(CHUNKS):
            for dx in range(NX):
                for s in range(2):
                    qmat[pl.ds((dx * 2 + s) * GSRC, GSRC), j * LANES : (j + 1) * LANES] = tall[
                        pl.ds(dx * GSRC * 16 + s * 8 + j, GSRC, stride=16), :
                    ].astype(BF)

        tops = []
        for b in range(6):
            scores = lax.dot_general(
                dense[b], qmat[...], (((1,), (1,)), ((), ())), preferred_element_type=F32
            )
            tops.append(jnp.max(scores, axis=0, keepdims=True))
        maxima[g] = jnp.concatenate(tops + [jnp.zeros((2, LANES), F32)], axis=0)

    for p in range(4):
        forward(p)
    score(0)
    forward(4)
    forward(5)
    score(1)
    forward(6)
    forward(7)
    score(2)
    score(3)

    lane = iota((8, LANES), 1)
    for dx in range(NX):
        total = jnp.zeros((8, LANES), F32)
        for g in range(GROUPS):
            turned = pltpu.roll(maxima[g], ((g - dx) * 32) % LANES, 1) if g != dx else maxima[g]
            total = jnp.where(lane // 32 == g, turned, total)
        if dx == 0:
            xback[0] = total
        else:
            back[dx] = total
    xbacks = [
        pltpu.make_async_remote_copy(
            src_ref=back.at[dx], dst_ref=xback.at[dx], send_sem=xb_send.at[dx - 1], recv_sem=xb_recv.at[dx - 1],
            device_id=beside(NX - dx), device_id_type=MESH,
        )
        for dx in range(1, NX)
    ]
    for copy in xbacks:
        copy.start()
    for copy in xbacks:
        copy.wait_recv()
    wide = jnp.concatenate([xback[...].reshape(NX * 8, LANES), jnp.zeros((LANES - NX * 8, LANES), F32)], axis=0)
    slots = wide.T
    for g in range(GROUPS):
        first = slots[g * 32 : g * 32 + 16, :]
        second = slots[g * 32 + 16 : g * 32 + 32, :]
        ret_src[group(g), 0, :] = first + pltpu.roll(second, 64, 1)
    ret_dst[0] = ret_src[0]

    def give_back(i, carry):
        pltpu.make_async_remote_copy(
            src_ref=ret_src.at[i], dst_ref=ret_dst.at[i], send_sem=ret_send, recv_sem=ret_recv,
            device_id=(behind(l, i), q), device_id_type=MESH,
        ).start()
        return carry

    lax.fori_loop(1, NL, give_back, 0)

    window = to_column(window_ref[...].astype(F32)).astype(I32)
    lanes = []
    for k in range(8):
        block_id = window + k
        r, col = block_id // 8, block_id % 8
        dx = (col // 2 - x + NX) % NX
        slot = jnp.where(r == 0, 1, jnp.where(r == 1, 0, 2))
        row = jnp.where(col % 2 == core, slot, 3 + slot)
        out_of_range = ((owner == 0) & (r == 0)) | ((owner == NL - 1) & (r == 2))
        target = dx * 8 + row + turn.astype(I32) * 64
        lanes.append(jnp.where(out_of_range, -1, target))
    take = jnp.where(iota((ROWS, NL), 1) == place.astype(I32), 1.0, 0.0)

    others = pl.ds(1, NL - 1)
    pltpu.make_async_copy(ret_dst.at[others], ret_dst.at[others], ret_recv).wait()
    mine = jnp.dot(take, ret_dst[:, 0, :], precision=lax.Precision.HIGHEST, preferred_element_type=F32)
    result = jnp.zeros((ROWS, LANES), F32)
    for k in range(8):
        value = jnp.sum(jnp.where(iota((ROWS, LANES), 1) == lanes[k], mine, 0.0), axis=1, keepdims=True)
        result = jnp.where(iota((ROWS, LANES), 1) == k, value, result)
    out_ref[...] = result.T[0:8, :]

    for copy in raw:
        copy.wait_send()
    for copy in mates:
        copy.wait_send()
    for copies in forwards:
        for copy in copies:
            copy.wait_send()
    for copy in xbacks:
        copy.wait_send()
    pltpu.make_async_copy(outgoing.at[others], outgoing.at[others], a2a_send).wait()
    pltpu.make_async_copy(ret_src.at[others], ret_src.at[others], ret_send).wait()


def per_device(queries, owner, window_start, peak_bins, peak_int, block_shift):
    dma = pltpu.SemaphoreType.DMA
    hbm = pl.BlockSpec(memory_space=pltpu.HBM)
    return pl.pallas_call(
        kernel,
        out_shape=jax.ShapeDtypeStruct((8, ROWS), F32),
        in_specs=[hbm] * 5 + [pl.BlockSpec(memory_space=pltpu.SMEM)],
        out_specs=pl.BlockSpec(memory_space=pltpu.VMEM),
        scratch_shapes=[
            pltpu.VMEM((ROWS, B), BF),
            pltpu.VMEM((1, ROWS), I32),
            pltpu.VMEM((1, ROWS), I32),
            pltpu.VMEM((CB, LANES), I32),
            pltpu.VMEM((3, CB, LANES), jnp.int16),
            pltpu.VMEM((3, CB, LANES), BF),
            pltpu.VMEM((3, 8, LANES), I32),
            dma((5,)),
            pltpu.VMEM((1024, LANES), F32),
            pltpu.VMEM((NL, 16, LANES), BF),
            pltpu.VMEM((NX, NL, 16, LANES), BF),
            pltpu.VMEM((LANES, B), BF),
            pltpu.VMEM((CB, 2 * LANES), F32),
            pltpu.VMEM((CB, 2 * LANES), F32),
            pltpu.VMEM((CB, 2 * LANES), F32),
            pltpu.VMEM((6, CB, B), BF),
            pltpu.VMEM((GROUPS, 8, LANES), F32),
            pltpu.VMEM((NX, 8, LANES), F32),
            pltpu.VMEM((NX, 8, LANES), F32),
            pltpu.VMEM((NL, 1, LANES), F32),
            pltpu.VMEM((NL, 1, LANES), F32),
            dma((2, 3)), dma((2, 3)),
            dma((3,)), dma((3,)),
            dma, dma((PIECES,)),
            dma((PIECES, NX - 1)), dma((PIECES, NX - 1)),
            dma((NX - 1,)), dma((NX - 1,)),
            dma, dma,
        ],
        compiler_params=pltpu.CompilerParams(
            collective_id=0, has_side_effects=True, vmem_limit_bytes=60 * 1024 * 1024
        ),
    )(
        queries, owner.reshape(1, ROWS), window_start.reshape(1, ROWS), peak_bins, peak_int,
        block_shift,
    ).T


def solution(mesh):
    both = ("lib", "qry")
    placed = (P(both, None), P(both, None), P(both), P(both, None), P(both, None), P(both))
    return jax.shard_map(
        per_device, mesh=mesh, in_specs=placed, out_specs=P(both, None), check_vma=False
    )
```

```python
import jax
import jax.numpy as jnp
from jax import lax
from jax.experimental import pallas as pl
from jax.experimental.pallas import tpu as pltpu
from jax.sharding import PartitionSpec as P

MESH = pl.DeviceIdType.MESH
B = 1024
NZ, NY, NX = 16, 4, 4
NL = NZ * NY
ROWS = 64
CB = 128
LANES = 128
CHUNKS = B // LANES
HALVES = 2
HSRC = NL // HALVES
PIECES = 8
PSRC = NL // PIECES
DZS = (8, 7, 9, 6, 10, 5, 11, 4, 12, 3, 13, 2, 14, 1, 15, 0)
DYS = (2, 1, 3, 0)
OFFSETS = [(dz, dy) for dz in DZS for dy in DYS]
HIS, LOS = 16, 64
UNROLL = 32
BF, F32, I32 = jnp.bfloat16, jnp.float32, jnp.int32


def iota(shape, axis):
    return lax.broadcasted_iota(I32, shape, axis)


def place_of(owner, l):
    dz = (owner // NY - l // NY + NZ) % NZ
    dy = (owner % NY - l % NY + NY) % NY
    k = jnp.where(dz == 0, NZ - 1, jnp.where(dz < 8, 15 - 2 * dz, jnp.where(dz == 8, 0, 2 * dz - 16)))
    return k * NY + jnp.where(dy == 0, 3, jnp.where(dy == 3, 2, jnp.where(dy == 1, 1, 0)))


def to_row(column):
    n = column.shape[0]
    return jnp.sum(jnp.where(iota((n, n), 0) == iota((n, n), 1), column, 0.0), axis=0, keepdims=True)


def to_column(row):
    n = row.shape[1]
    return jnp.sum(jnp.where(iota((n, n), 0) == iota((n, n), 1), row, 0.0), axis=1, keepdims=True)


def kernel(
    q_hbm, owner_hbm, window_hbm, bins_hbm, int_hbm, shift_smem,
    out_ref,
    q_ref, owner_ref, window_ref, peaks_ref, bins_ref, int_ref, shift_ref, load_sem,
    tall, outgoing, qbuf, qmat, hi_ref, lo_ref, w_ref, dense, back, xback, ret_src, ret_dst,
    raw_send, raw_recv, mate_send, mate_recv, a2a_send, a2a_recv, fwd_send, fwd_recv, xb_send, xb_recv,
    ret_send, ret_recv,
):
    l, q = lax.axis_index("lib"), lax.axis_index("qry")
    x, core = q // 2, q % 2
    mate = (l, x * 2 + 1 - core)
    along_z = [lax.rem(l // NY + dz, NZ) * NY for dz in range(NZ)]
    along_y = [lax.rem(l % NY + dy, NY) for dy in range(NY)]

    def ahead(i):
        dz, dy = OFFSETS[i]
        return (along_z[dz] + along_y[dy], q)

    def behind(i):
        dz, dy = OFFSETS[i]
        return (along_z[-dz % NZ] + along_y[-dy % NY], q)

    def beside(dx):
        return (l, lax.rem(x + dx, NX) * 2 + core)

    loads = [
        pltpu.make_async_copy(src, dst, load_sem.at[i])
        for i, (src, dst) in enumerate(
            (
                (owner_hbm, owner_ref),
                (q_hbm, q_ref),
                (window_hbm, window_ref),
                (bins_hbm, peaks_ref),
                (int_hbm, int_ref.at[0]),
            )
        )
    ]
    for load in loads:
        load.start()

    barrier = pltpu.get_barrier_semaphore()

    for i in range(NL - 1):
        pl.semaphore_signal(barrier, inc=1, device_id=ahead(i), device_id_type=MESH)
    for dx in range(1, NX):
        pl.semaphore_signal(barrier, inc=1, device_id=beside(dx), device_id_type=MESH)
    pl.semaphore_signal(barrier, inc=1, device_id=mate, device_id_type=MESH)
    for load in loads[:2]:
        load.wait()

    owner_row = owner_ref[...].astype(F32)
    owner_col = to_column(owner_row)
    owner = owner_col.astype(I32)
    square = (ROWS, ROWS)
    earlier = (owner_col == owner_row) & (iota(square, 1) < iota(square, 0))
    turn = jnp.sum(jnp.where(earlier, 1.0, 0.0), axis=1, keepdims=True)
    place = place_of(owner, l).astype(F32)
    slot_row = to_row(place * 2.0 + turn)
    pick = jnp.where(iota((2 * NL, ROWS), 0).astype(F32) == slot_row, 1.0, 0.0).astype(BF)
    rows = jnp.dot(pick, q_ref[...], preferred_element_type=F32)
    for j in range(CHUNKS):
        tall[pl.ds(j, 2 * NL, stride=CHUNKS), :] = rows[:, j * LANES : (j + 1) * LANES]
    outgoing[...] = tall[0 : NL * 16, :].astype(BF).reshape(NL, 16, LANES)
    qbuf[0, NL - 1] = outgoing[NL - 1]

    def densify(r):
        bins, weights = bins_ref[r].astype(I32), int_ref[r].astype(F32)
        moved = bins + shift_ref[r, 0:1, :]
        hi_ref[:, 0:LANES] = (bins >> 6).astype(F32)
        hi_ref[:, LANES:] = (moved >> 6).astype(F32)
        lo_ref[:, 0:LANES] = (bins & (LOS - 1)).astype(F32)
        lo_ref[:, LANES:] = (moved & (LOS - 1)).astype(F32)
        w_ref[:, 0:LANES] = weights
        w_ref[:, LANES:] = weights
        hi_ids = iota((HIS, 2 * LANES), 0).astype(F32)
        lo_ids = iota((LOS, 2 * LANES), 0).astype(F32)
        left = iota((HIS, LANES), 1) < LOS

        def some(i, carry):
            at = pl.ds(pl.multiple_of(i * UNROLL, UNROLL), UNROLL)
            his, los, ws = hi_ref[at, :], lo_ref[at, :], w_ref[at, :]
            for c in range(0, UNROLL, 2):
                a = [jnp.where(hi_ids == his[e : e + 1, :], ws[e : e + 1, :], 0.0).astype(BF) for e in (c, c + 1)]
                b = [jnp.where(lo_ids == los[e : e + 1, :], 1.0, 0.0).astype(BF) for e in (c, c + 1)]
                d = lax.dot_general(
                    jnp.concatenate(a, 0), jnp.concatenate(b, 0), (((1,), (1,)), ((), ())),
                    preferred_element_type=F32,
                )
                row = pl.multiple_of(i * (UNROLL * 8), UNROLL * 8) + c * 8
                tall[pl.ds(row, HIS), :] = jnp.where(left, d[:HIS], d[HIS:])
            return carry

        lax.fori_loop(0, CB // UNROLL, some, 0)
        half = iota((CB // 2, LANES), 1) < LOS
        for j in range(CHUNKS):
            e = tall[pl.ds(2 * j, CB // 2, stride=HIS), :]
            f = tall[pl.ds(2 * j + 1, CB // 2, stride=HIS), :]
            at = slice(j * LANES, (j + 1) * LANES)
            dense[r, 0 : CB // 2, at] = jnp.where(half, e, pltpu.roll(f, LOS, 1)).astype(BF)
            dense[r, CB // 2 :, at] = jnp.where(half, pltpu.roll(e, LOS, 1), f).astype(BF)

    def to_mate(r):
        return pltpu.make_async_remote_copy(
            src_ref=dense.at[r], dst_ref=dense.at[3 + r], send_sem=mate_send.at[r], recv_sem=mate_recv.at[r],
            device_id=mate, device_id_type=MESH,
        )

    for load in loads[2:]:
        load.wait()
    bins_ref[0] = peaks_ref[...].astype(jnp.int16)
    shift_ref[0] = jnp.full((8, LANES), shift_smem[0], I32)
    densify(0)
    pl.semaphore_wait(barrier, NL - 1 + NX - 1 + 1)

    raw = []
    for slot, to in ((1, lax.rem(l + 1, NL)), (2, lax.rem(l + NL - 1, NL))):
        for i, ref in enumerate((bins_ref, int_ref, shift_ref)):
            raw.append(
                pltpu.make_async_remote_copy(
                    src_ref=ref.at[0], dst_ref=ref.at[slot], send_sem=raw_send.at[slot - 1, i],
                    recv_sem=raw_recv.at[slot - 1, i], device_id=(to, q), device_id_type=MESH,
                )
            )
    for copy in raw:
        copy.start()

    for i in range(NL - 1):
        pltpu.make_async_remote_copy(
            src_ref=outgoing.at[i], dst_ref=qbuf.at[0, i], send_sem=a2a_send, recv_sem=a2a_recv.at[i // PSRC],
            device_id=ahead(i), device_id_type=MESH,
        ).start()
    mates = [to_mate(0)]
    mates[0].start()
    for slot in (1, 2):
        for i in range(3):
            raw[(slot - 1) * 3 + i].wait_recv()
        densify(slot)
        mates.append(to_mate(slot))
        mates[slot].start()

    forwards = []

    def forward(p):
        piece = pl.ds(p * PSRC, PSRC)
        arrived = qbuf.at[0, pl.ds(p * PSRC, PSRC - 1) if p == PIECES - 1 else piece]
        pltpu.make_async_copy(arrived, arrived, a2a_recv.at[p]).wait()
        copies = [
            pltpu.make_async_remote_copy(
                src_ref=qbuf.at[0, piece], dst_ref=qbuf.at[dx, piece], send_sem=fwd_send.at[p, dx - 1],
                recv_sem=fwd_recv.at[p, dx - 1], device_id=beside(dx), device_id_type=MESH,
            )
            for dx in range(1, NX)
        ]
        for copy in copies:
            copy.start()
        forwards.append(copies)

    def score(h):
        for copies in forwards[h * PIECES // HALVES : (h + 1) * PIECES // HALVES]:
            for copy in copies:
                copy.wait_recv()
        for dx in range(NX):
            part = qbuf[dx, pl.ds(h * HSRC, HSRC)].reshape(HSRC * 16, LANES)
            tall[pl.ds(dx * HSRC * 16, HSRC * 16), :] = part.astype(F32)
        for j in range(CHUNKS):
            for dx in range(NX):
                for s in range(2):
                    qmat[pl.ds((dx * 2 + s) * HSRC, HSRC), j * LANES : (j + 1) * LANES] = tall[
                        pl.ds(dx * HSRC * 16 + s * 8 + j, HSRC, stride=16), :
                    ].astype(BF)
        tops = []
        for b in range(6):
            scores = lax.dot_general(
                dense[b], qmat[...], (((1,), (1,)), ((), ())), preferred_element_type=F32
            )
            tops.append(jnp.max(scores, axis=0, keepdims=True))
        return jnp.concatenate(tops + [jnp.zeros((2, NX * 2 * HSRC), F32)], axis=0)

    xbacks = []

    def back_along_x(h, maxima):
        copies = []
        for dx in range(NX):
            part = maxima[:, dx // 2 * LANES : dx // 2 * LANES + LANES]
            part = pltpu.roll(part, LANES // 2, 1) if dx % 2 else part
            if dx == 0:
                xback[h, 0] = part
            else:
                back[h, dx] = part
                copies.append(
                    pltpu.make_async_remote_copy(
                        src_ref=back.at[h, dx], dst_ref=xback.at[h, dx], send_sem=xb_send.at[h, dx - 1],
                        recv_sem=xb_recv.at[h, dx - 1], device_id=beside(NX - dx), device_id_type=MESH,
                    )
                )
        for copy in copies:
            copy.start()
        xbacks.append(copies)

    def back_along_lib(h):
        for copy in xbacks[h]:
            copy.wait_recv()
        wide = jnp.concatenate(
            [xback[h].reshape(NX * 8, LANES), jnp.zeros((LANES - NX * 8, LANES), F32)], axis=0
        ).T
        ret_src[pl.ds(h * HSRC, HSRC), 0, :] = wide[0:HSRC] + pltpu.roll(wide[HSRC : 2 * HSRC], LANES // 2, 1)
        for i in range(h * HSRC, min((h + 1) * HSRC, NL - 1)):
            pltpu.make_async_remote_copy(
                src_ref=ret_src.at[i], dst_ref=ret_dst.at[i], send_sem=ret_send, recv_sem=ret_recv,
                device_id=behind(i), device_id_type=MESH,
            ).start()

    for p in range(PIECES):
        forward(p)
    for copy in mates:
        copy.wait_recv()
    back_along_x(0, score(0))
    back_along_x(1, score(1))
    back_along_lib(0)
    back_along_lib(1)
    ret_dst[NL - 1] = ret_src[NL - 1]

    window = to_column(window_ref[...].astype(F32)).astype(I32)
    lanes = []
    for k in range(8):
        block_id = window + k
        r, col = block_id // 8, block_id % 8
        dx = (col // 2 - x + NX) % NX
        slot = jnp.where(r == 0, 1, jnp.where(r == 1, 0, 2))
        row = jnp.where(col % 2 == core, slot, 3 + slot)
        out_of_range = ((owner == 0) & (r == 0)) | ((owner == NL - 1) & (r == 2))
        target = dx * 8 + row + turn.astype(I32) * 64
        lanes.append(jnp.where(out_of_range, -1, target))
    take = jnp.where(iota((ROWS, NL), 1) == place.astype(I32), 1.0, 0.0)

    others = pl.ds(0, NL - 1)
    pltpu.make_async_copy(ret_dst.at[others], ret_dst.at[others], ret_recv).wait()
    mine = jnp.dot(take, ret_dst[:, 0, :], precision=lax.Precision.HIGHEST, preferred_element_type=F32)
    result = jnp.zeros((ROWS, LANES), F32)
    for k in range(8):
        value = jnp.sum(jnp.where(iota((ROWS, LANES), 1) == lanes[k], mine, 0.0), axis=1, keepdims=True)
        result = jnp.where(iota((ROWS, LANES), 1) == k, value, result)
    out_ref[...] = result[:, 0:8]

    for copy in raw:
        copy.wait_send()
    for copy in mates:
        copy.wait_send()
    for copies in forwards:
        for copy in copies:
            copy.wait_send()
    for copies in xbacks:
        for copy in copies:
            copy.wait_send()
    pltpu.make_async_copy(outgoing.at[others], outgoing.at[others], a2a_send).wait()
    pltpu.make_async_copy(ret_src.at[others], ret_src.at[others], ret_send).wait()


def per_device(queries, owner, window_start, peak_bins, peak_int, block_shift):
    dma = pltpu.SemaphoreType.DMA
    hbm = pl.BlockSpec(memory_space=pltpu.HBM)
    return pl.pallas_call(
        kernel,
        out_shape=pltpu.VMEM((ROWS, 8), F32),
        in_specs=[hbm] * 5 + [pl.BlockSpec(memory_space=pltpu.SMEM)],
        out_specs=pl.BlockSpec(memory_space=pltpu.VMEM),
        scratch_shapes=[
            pltpu.VMEM((ROWS, B), BF),
            pltpu.VMEM((1, ROWS), I32),
            pltpu.VMEM((1, ROWS), I32),
            pltpu.VMEM((CB, LANES), I32),
            pltpu.VMEM((3, CB, LANES), jnp.int16),
            pltpu.VMEM((3, CB, LANES), BF),
            pltpu.VMEM((3, 8, LANES), I32),
            dma((5,)),
            pltpu.VMEM((2048, LANES), F32),
            pltpu.VMEM((NL, 16, LANES), BF),
            pltpu.VMEM((NX, NL, 16, LANES), BF),
            pltpu.VMEM((NX * 2 * HSRC, B), BF),
            pltpu.VMEM((CB, 2 * LANES), F32),
            pltpu.VMEM((CB, 2 * LANES), F32),
            pltpu.VMEM((CB, 2 * LANES), F32),
            pltpu.VMEM((6, CB, B), BF),
            pltpu.VMEM((HALVES, NX, 8, LANES), F32),
            pltpu.VMEM((HALVES, NX, 8, LANES), F32),
            pltpu.VMEM((NL, 1, LANES), F32),
            pltpu.VMEM((NL, 1, LANES), F32),
            dma((2, 3)), dma((2, 3)),
            dma((3,)), dma((3,)),
            dma, dma((PIECES,)),
            dma((PIECES, NX - 1)), dma((PIECES, NX - 1)),
            dma((HALVES, NX - 1)), dma((HALVES, NX - 1)),
            dma, dma,
        ],
        compiler_params=pltpu.CompilerParams(
            collective_id=0, has_side_effects=True, vmem_limit_bytes=60 * 1024 * 1024
        ),
    )(
        queries, owner.reshape(1, ROWS), window_start.reshape(1, ROWS), peak_bins, peak_int,
        block_shift,
    )


def solution(mesh):
    both = ("lib", "qry")
    placed = (P(both, None), P(both, None), P(both), P(both, None), P(both, None), P(both))
    return jax.shard_map(
        per_device, mesh=mesh, in_specs=placed, out_specs=P(both, None), check_vma=False
    )
```

```python
import jax
import jax.numpy as jnp
from jax import lax
from jax.experimental import pallas as pl
from jax.experimental.pallas import tpu as pltpu
from jax.sharding import PartitionSpec as P

MESH = pl.DeviceIdType.MESH
B = 1024
NZ, NY, NX = 16, 4, 4
NL = NZ * NY
ROWS = 64
CB = 128
LANES = 128
CHUNKS = B // LANES
HALVES = 2
HSRC = NL // HALVES
PIECES = 8
PSRC = NL // PIECES
DZS = (8, 7, 9, 6, 10, 5, 11, 4, 12, 3, 13, 2, 14, 1, 15, 0)
DYS = (2, 1, 3, 0)
OFFSETS = [(dz, dy) for dz in DZS for dy in DYS]
HIS, LOS = 16, 64
UNROLL = 32
BF, F32, I32 = jnp.bfloat16, jnp.float32, jnp.int32


def iota(shape, axis):
    return lax.broadcasted_iota(I32, shape, axis)


def place_of(owner, l):
    dz = (owner // NY - l // NY + NZ) % NZ
    dy = (owner % NY - l % NY + NY) % NY
    k = jnp.where(dz == 0, NZ - 1, jnp.where(dz < 8, 15 - 2 * dz, jnp.where(dz == 8, 0, 2 * dz - 16)))
    return k * NY + jnp.where(dy == 0, 3, jnp.where(dy == 3, 2, jnp.where(dy == 1, 1, 0)))


def to_row(column):
    n = column.shape[0]
    return jnp.sum(jnp.where(iota((n, n), 0) == iota((n, n), 1), column, 0.0), axis=0, keepdims=True)


def to_column(row):
    n = row.shape[1]
    return jnp.sum(jnp.where(iota((n, n), 0) == iota((n, n), 1), row, 0.0), axis=1, keepdims=True)


def kernel(
    q_hbm, owner_hbm, window_hbm, bins_hbm, int_hbm, shift_smem,
    out_ref,
    q_ref, owner_ref, window_ref, peaks_ref, bins_ref, int_ref, shift_ref, load_sem,
    tall, outgoing, qbuf, qmat, hi_ref, lo_ref, w_ref, dense, back, xback, ret_src, ret_dst,
    raw_send, raw_recv, mate_send, mate_recv, a2a_send, a2a_recv, fwd_send, fwd_recv, xb_send, xb_recv,
    ret_send, ret_recv,
):
    l, q = lax.axis_index("lib"), lax.axis_index("qry")
    x, core = q // 2, q % 2
    mate = (l, x * 2 + 1 - core)
    along_z = [lax.rem(l // NY + dz, NZ) * NY for dz in range(NZ)]
    along_y = [lax.rem(l % NY + dy, NY) for dy in range(NY)]

    def ahead(i):
        dz, dy = OFFSETS[i]
        return (along_z[dz] + along_y[dy], q)

    def behind(i):
        dz, dy = OFFSETS[i]
        return (along_z[-dz % NZ] + along_y[-dy % NY], q)

    def beside(dx):
        return (l, lax.rem(x + dx, NX) * 2 + core)

    loads = [
        pltpu.make_async_copy(src, dst, load_sem.at[i])
        for i, (src, dst) in enumerate(
            (
                (owner_hbm, owner_ref),
                (q_hbm, q_ref),
                (window_hbm, window_ref),
                (bins_hbm, peaks_ref),
                (int_hbm, int_ref.at[0]),
            )
        )
    ]
    for load in loads:
        load.start()

    barrier = pltpu.get_barrier_semaphore()

    for i in range(NL - 1):
        pl.semaphore_signal(barrier, inc=1, device_id=ahead(i), device_id_type=MESH)
    for dx in range(1, NX):
        pl.semaphore_signal(barrier, inc=1, device_id=beside(dx), device_id_type=MESH)

    @pl.when(core == 0)
    def _():
        pl.semaphore_signal(barrier, inc=1, device_id=mate, device_id_type=MESH)

    for load in loads[:2]:
        load.wait()

    owner_row = owner_ref[...].astype(F32)
    owner_col = to_column(owner_row)
    owner = owner_col.astype(I32)
    square = (ROWS, ROWS)
    earlier = (owner_col == owner_row) & (iota(square, 1) < iota(square, 0))
    turn = jnp.sum(jnp.where(earlier, 1.0, 0.0), axis=1, keepdims=True)
    place = place_of(owner, l).astype(F32)
    slot_row = to_row(place * 2.0 + turn)
    pick = jnp.where(iota((2 * NL, ROWS), 0).astype(F32) == slot_row, 1.0, 0.0).astype(BF)
    rows = jnp.dot(pick, q_ref[...], preferred_element_type=F32)
    for j in range(CHUNKS):
        tall[pl.ds(j, 2 * NL, stride=CHUNKS), :] = rows[:, j * LANES : (j + 1) * LANES]
    outgoing[...] = tall[0 : NL * 16, :].astype(BF).reshape(NL, 16, LANES)
    qbuf[0, NL - 1] = outgoing[NL - 1]

    def densify(r):
        bins, weights = bins_ref[r].astype(I32), int_ref[r].astype(F32)
        moved = bins + shift_ref[r, 0:1, :]
        hi_ref[:, 0:LANES] = (bins >> 6).astype(F32)
        hi_ref[:, LANES:] = (moved >> 6).astype(F32)
        lo_ref[:, 0:LANES] = (bins & (LOS - 1)).astype(F32)
        lo_ref[:, LANES:] = (moved & (LOS - 1)).astype(F32)
        w_ref[:, 0:LANES] = weights
        w_ref[:, LANES:] = weights
        hi_ids = iota((HIS, 2 * LANES), 0).astype(F32)
        lo_ids = iota((LOS, 2 * LANES), 0).astype(F32)
        left = iota((HIS, LANES), 1) < LOS

        def some(i, carry):
            at = pl.ds(pl.multiple_of(i * UNROLL, UNROLL), UNROLL)
            his, los, ws = hi_ref[at, :], lo_ref[at, :], w_ref[at, :]
            for c in range(0, UNROLL, 2):
                a = [jnp.where(hi_ids == his[e : e + 1, :], ws[e : e + 1, :], 0.0).astype(BF) for e in (c, c + 1)]
                b = [jnp.where(lo_ids == los[e : e + 1, :], 1.0, 0.0).astype(BF) for e in (c, c + 1)]
                d = lax.dot_general(
                    jnp.concatenate(a, 0), jnp.concatenate(b, 0), (((1,), (1,)), ((), ())),
                    preferred_element_type=F32,
                )
                row = pl.multiple_of(i * (UNROLL * 8), UNROLL * 8) + c * 8
                tall[pl.ds(row, HIS), :] = jnp.where(left, d[:HIS], d[HIS:])
            return carry

        lax.fori_loop(0, CB // UNROLL, some, 0)
        half = iota((CB // 2, LANES), 1) < LOS
        for j in range(CHUNKS):
            e = tall[pl.ds(2 * j, CB // 2, stride=HIS), :]
            f = tall[pl.ds(2 * j + 1, CB // 2, stride=HIS), :]
            at = slice(j * LANES, (j + 1) * LANES)
            dense[r, 0 : CB // 2, at] = jnp.where(half, e, pltpu.roll(f, LOS, 1)).astype(BF)
            dense[r, CB // 2 :, at] = jnp.where(half, pltpu.roll(e, LOS, 1), f).astype(BF)

    def to_mate(r):
        return pltpu.make_async_remote_copy(
            src_ref=dense.at[r], dst_ref=dense.at[3 + r], send_sem=mate_send.at[r], recv_sem=mate_recv.at[r],
            device_id=mate, device_id_type=MESH,
        )

    for load in loads[2:]:
        load.wait()
    bins_ref[0] = peaks_ref[...].astype(jnp.int16)
    shift_ref[0] = jnp.full((8, LANES), shift_smem[0], I32)
    densify(0)
    pl.semaphore_wait(barrier, NL - 1 + NX - 1 + core)

    raw = []
    for slot, to in ((1, lax.rem(l + 1, NL)), (2, lax.rem(l + NL - 1, NL))):
        for i, ref in enumerate((bins_ref, int_ref, shift_ref)):
            raw.append(
                pltpu.make_async_remote_copy(
                    src_ref=ref.at[0], dst_ref=ref.at[slot], send_sem=raw_send.at[slot - 1, i],
                    recv_sem=raw_recv.at[slot - 1, i], device_id=(to, q), device_id_type=MESH,
                )
            )
    for copy in raw:
        copy.start()

    for i in range(NL - 1):
        pltpu.make_async_remote_copy(
            src_ref=outgoing.at[i], dst_ref=qbuf.at[0, i], send_sem=a2a_send, recv_sem=a2a_recv.at[i // PSRC],
            device_id=ahead(i), device_id_type=MESH,
        ).start()
    mates = [to_mate(r) for r in range(3)]

    @pl.when(core == 1)
    def _():
        mates[0].start()

    for slot in (1, 2):
        for i in range(3):
            raw[(slot - 1) * 3 + i].wait_recv()
        densify(slot)

        @pl.when(core == 1)
        def _():
            mates[slot].start()


    forwards = []

    def forward(p):
        piece = pl.ds(p * PSRC, PSRC)
        arrived = qbuf.at[0, pl.ds(p * PSRC, PSRC - 1) if p == PIECES - 1 else piece]
        pltpu.make_async_copy(arrived, arrived, a2a_recv.at[p]).wait()
        copies = [
            pltpu.make_async_remote_copy(
                src_ref=qbuf.at[0, piece], dst_ref=qbuf.at[dx, piece], send_sem=fwd_send.at[p, dx - 1],
                recv_sem=fwd_recv.at[p, dx - 1], device_id=beside(dx), device_id_type=MESH,
            )
            for dx in range(1, NX)
        ]
        for copy in copies:
            copy.start()
        forwards.append(copies)

    def score(h):
        for copies in forwards[h * PIECES // HALVES : (h + 1) * PIECES // HALVES]:
            for copy in copies:
                copy.wait_recv()
        for dx in range(NX):
            part = qbuf[dx, pl.ds(h * HSRC, HSRC)].reshape(HSRC * 16, LANES)
            tall[pl.ds(dx * HSRC * 16, HSRC * 16), :] = part.astype(F32)
        for j in range(CHUNKS):
            for dx in range(NX):
                for s in range(2):
                    qmat[pl.ds((dx * 2 + s) * HSRC, HSRC), j * LANES : (j + 1) * LANES] = tall[
                        pl.ds(dx * HSRC * 16 + s * 8 + j, HSRC, stride=16), :
                    ].astype(BF)
        tops = []
        for b in range(6):
            if h == 0 and b == 3:

                @pl.when(core == 1)
                def _():
                    mates[0].wait_recv()

                for copy in mates[1:]:
                    copy.wait_recv()
            scores = lax.dot_general(
                dense[b], qmat[...], (((1,), (1,)), ((), ())), preferred_element_type=F32
            )
            tops.append(jnp.max(scores, axis=0, keepdims=True))
        return jnp.concatenate(tops + [jnp.zeros((2, NX * 2 * HSRC), F32)], axis=0)

    xbacks = []

    def back_along_x(h, maxima):
        copies = []
        for dx in range(NX):
            part = maxima[:, dx // 2 * LANES : dx // 2 * LANES + LANES]
            part = pltpu.roll(part, LANES // 2, 1) if dx % 2 else part
            if dx == 0:
                xback[h, 0] = part
            else:
                back[h, dx] = part
                copies.append(
                    pltpu.make_async_remote_copy(
                        src_ref=back.at[h, dx], dst_ref=xback.at[h, dx], send_sem=xb_send.at[h, dx - 1],
                        recv_sem=xb_recv.at[h, dx - 1], device_id=beside(NX - dx), device_id_type=MESH,
                    )
                )
        for copy in copies:
            copy.start()
        xbacks.append(copies)

    def back_along_lib(h):
        for copy in xbacks[h]:
            copy.wait_recv()
        wide = jnp.concatenate(
            [xback[h].reshape(NX * 8, LANES), jnp.zeros((LANES - NX * 8, LANES), F32)], axis=0
        ).T
        ret_src[pl.ds(h * HSRC, HSRC), 0, :] = wide[0:HSRC] + pltpu.roll(wide[HSRC : 2 * HSRC], LANES // 2, 1)
        for i in range(h * HSRC, min((h + 1) * HSRC, NL - 1)):
            pltpu.make_async_remote_copy(
                src_ref=ret_src.at[i], dst_ref=ret_dst.at[i], send_sem=ret_send, recv_sem=ret_recv,
                device_id=behind(i), device_id_type=MESH,
            ).start()

    for p in range(PIECES):
        forward(p)
        if p == PIECES // 2 - 1:

            @pl.when(core == 0)
            def _():
                mates[0].wait_recv()
                for copy in mates:
                    copy.start()

    back_along_x(0, score(0))
    back_along_x(1, score(1))
    back_along_lib(0)
    back_along_lib(1)
    ret_dst[NL - 1] = ret_src[NL - 1]

    window = to_column(window_ref[...].astype(F32)).astype(I32)
    lanes = []
    for k in range(8):
        block_id = window + k
        r, col = block_id // 8, block_id % 8
        dx = (col // 2 - x + NX) % NX
        slot = jnp.where(r == 0, 1, jnp.where(r == 1, 0, 2))
        row = jnp.where(col % 2 == core, slot, 3 + slot)
        out_of_range = ((owner == 0) & (r == 0)) | ((owner == NL - 1) & (r == 2))
        target = dx * 8 + row + turn.astype(I32) * 64
        lanes.append(jnp.where(out_of_range, -1, target))
    take = jnp.where(iota((ROWS, NL), 1) == place.astype(I32), 1.0, 0.0)

    others = pl.ds(0, NL - 1)
    pltpu.make_async_copy(ret_dst.at[others], ret_dst.at[others], ret_recv).wait()
    mine = jnp.dot(take, ret_dst[:, 0, :], precision=lax.Precision.HIGHEST, preferred_element_type=F32)
    result = jnp.zeros((ROWS, LANES), F32)
    for k in range(8):
        value = jnp.sum(jnp.where(iota((ROWS, LANES), 1) == lanes[k], mine, 0.0), axis=1, keepdims=True)
        result = jnp.where(iota((ROWS, LANES), 1) == k, value, result)
    out_ref[...] = result[:, 0:8]

    for copy in raw:
        copy.wait_send()
    for copy in mates:
        copy.wait_send()
    for copies in forwards:
        for copy in copies:
            copy.wait_send()
    for copies in xbacks:
        for copy in copies:
            copy.wait_send()
    pltpu.make_async_copy(outgoing.at[others], outgoing.at[others], a2a_send).wait()
    pltpu.make_async_copy(ret_src.at[others], ret_src.at[others], ret_send).wait()


def per_device(queries, owner, window_start, peak_bins, peak_int, block_shift):
    dma = pltpu.SemaphoreType.DMA
    hbm = pl.BlockSpec(memory_space=pltpu.HBM)
    return pl.pallas_call(
        kernel,
        out_shape=pltpu.VMEM((ROWS, 8), F32),
        in_specs=[hbm] * 5 + [pl.BlockSpec(memory_space=pltpu.SMEM)],
        out_specs=pl.BlockSpec(memory_space=pltpu.VMEM),
        scratch_shapes=[
            pltpu.VMEM((ROWS, B), BF),
            pltpu.VMEM((1, ROWS), I32),
            pltpu.VMEM((1, ROWS), I32),
            pltpu.VMEM((CB, LANES), I32),
            pltpu.VMEM((3, CB, LANES), jnp.int16),
            pltpu.VMEM((3, CB, LANES), BF),
            pltpu.VMEM((3, 8, LANES), I32),
            dma((5,)),
            pltpu.VMEM((2048, LANES), F32),
            pltpu.VMEM((NL, 16, LANES), BF),
            pltpu.VMEM((NX, NL, 16, LANES), BF),
            pltpu.VMEM((NX * 2 * HSRC, B), BF),
            pltpu.VMEM((CB, 2 * LANES), F32),
            pltpu.VMEM((CB, 2 * LANES), F32),
            pltpu.VMEM((CB, 2 * LANES), F32),
            pltpu.VMEM((6, CB, B), BF),
            pltpu.VMEM((HALVES, NX, 8, LANES), F32),
            pltpu.VMEM((HALVES, NX, 8, LANES), F32),
            pltpu.VMEM((NL, 1, LANES), F32),
            pltpu.VMEM((NL, 1, LANES), F32),
            dma((2, 3)), dma((2, 3)),
            dma((3,)), dma((3,)),
            dma, dma((PIECES,)),
            dma((PIECES, NX - 1)), dma((PIECES, NX - 1)),
            dma((HALVES, NX - 1)), dma((HALVES, NX - 1)),
            dma, dma,
        ],
        compiler_params=pltpu.CompilerParams(
            collective_id=0, has_side_effects=True, vmem_limit_bytes=60 * 1024 * 1024
        ),
    )(
        queries, owner.reshape(1, ROWS), window_start.reshape(1, ROWS), peak_bins, peak_int,
        block_shift,
    )


def solution(mesh):
    both = ("lib", "qry")
    placed = (P(both, None), P(both, None), P(both), P(both, None), P(both, None), P(both))
    return jax.shard_map(
        per_device, mesh=mesh, in_specs=placed, out_specs=P(both, None), check_vma=False
    )
```

```python
import jax
import jax.numpy as jnp
from jax import lax
from jax.experimental import pallas as pl
from jax.experimental.pallas import tpu as pltpu
from jax.sharding import PartitionSpec as P

MESH = pl.DeviceIdType.MESH
B = 1024
NZ, NY, NX = 16, 4, 4
NL = NZ * NY
ROWS = 64
CB = 128
LANES = 128
CHUNKS = B // LANES
BATCHES = 4
BSRC = NL // BATCHES
WIDTH = 2 * BSRC
PIECES = 8
PSRC = NL // PIECES
SCHEDULE = ("a0", "a1", "a2", "a3", "d0", "d1", "d2", "f0", "f1", "f2", "f3", "f4", "f5", "f6", "f7", "m", "s0", "s1", "s2", "s3")
DZS = (8, 7, 9, 6, 10, 5, 11, 4, 12, 3, 13, 2, 14, 1, 15, 0)
DYS = (2, 1, 3, 0)
OFFSETS = [(dz, dy) for dz in DZS for dy in DYS]
HIS, LOS = 16, 64
UNROLL = 32
BF, F32, I32 = jnp.bfloat16, jnp.float32, jnp.int32


def iota(shape, axis):
    return lax.broadcasted_iota(I32, shape, axis)


def place_of(owner, l):
    dz = (owner // NY - l // NY + NZ) % NZ
    dy = (owner % NY - l % NY + NY) % NY
    k = jnp.where(dz == 0, NZ - 1, jnp.where(dz < 8, 15 - 2 * dz, jnp.where(dz == 8, 0, 2 * dz - 16)))
    return k * NY + jnp.where(dy == 0, 3, jnp.where(dy == 3, 2, jnp.where(dy == 1, 1, 0)))


def to_row(column):
    n = column.shape[0]
    return jnp.sum(jnp.where(iota((n, n), 0) == iota((n, n), 1), column, 0.0), axis=0, keepdims=True)


def to_column(row):
    n = row.shape[1]
    return jnp.sum(jnp.where(iota((n, n), 0) == iota((n, n), 1), row, 0.0), axis=1, keepdims=True)


def kernel(
    q_hbm, owner_hbm, window_hbm, bins_hbm, int_hbm, shift_smem,
    out_ref,
    q_ref, owner_ref, window_ref, peaks_ref, bins_ref, int_ref, shift_ref, load_sem,
    tall, outgoing, qbuf, qmat, hi_ref, lo_ref, w_ref, dense, ret_src, ret_dst,
    raw_send, raw_recv, mate_send, mate_recv, a2a_send, a2a_recv, fwd_send, fwd_recv,
    ret_send, ret_recv,
):
    l, q = lax.axis_index("lib"), lax.axis_index("qry")
    x, core = q // 2, q % 2
    mate = (l, x * 2 + 1 - core)
    along_z = [lax.rem(l // NY + dz, NZ) * NY for dz in range(NZ)]
    along_y = [lax.rem(l % NY + dy, NY) for dy in range(NY)]

    def ahead(i):
        dz, dy = OFFSETS[i]
        return (along_z[dz] + along_y[dy], q)

    def behind(i):
        dz, dy = OFFSETS[i]
        return (along_z[-dz % NZ] + along_y[-dy % NY], q)

    def beside(dx):
        return (l, lax.rem(x + dx, NX) * 2 + core)

    loads = [
        pltpu.make_async_copy(src, dst, load_sem.at[i])
        for i, (src, dst) in enumerate(
            (
                (owner_hbm, owner_ref),
                (q_hbm, q_ref),
                (window_hbm, window_ref),
                (bins_hbm, peaks_ref),
                (int_hbm, int_ref.at[0]),
            )
        )
    ]
    for load in loads:
        load.start()

    barrier = pltpu.get_barrier_semaphore()

    for i in range(NL - 1):
        pl.semaphore_signal(barrier, inc=1, device_id=ahead(i), device_id_type=MESH)
    for dx in range(1, NX):
        pl.semaphore_signal(barrier, inc=1, device_id=beside(dx), device_id_type=MESH)

    @pl.when(core == 0)
    def _():
        pl.semaphore_signal(barrier, inc=1, device_id=mate, device_id_type=MESH)

    for load in loads[:2]:
        load.wait()

    owner_row = owner_ref[...].astype(F32)
    owner_col = to_column(owner_row)
    owner = owner_col.astype(I32)
    square = (ROWS, ROWS)
    earlier = (owner_col == owner_row) & (iota(square, 1) < iota(square, 0))
    turn = jnp.sum(jnp.where(earlier, 1.0, 0.0), axis=1, keepdims=True)
    place = place_of(owner, l).astype(F32)
    slot_row = to_row(place * 2.0 + turn)
    pick = jnp.where(iota((2 * NL, ROWS), 0).astype(F32) == slot_row, 1.0, 0.0).astype(BF)
    rows = jnp.dot(pick, q_ref[...], preferred_element_type=F32)
    for j in range(CHUNKS):
        tall[pl.ds(j, 2 * NL, stride=CHUNKS), :] = rows[:, j * LANES : (j + 1) * LANES]
    outgoing[...] = tall[0 : NL * 16, :].astype(BF).reshape(NL, 16, LANES)
    qbuf[0, NL - 1] = outgoing[NL - 1]

    def densify(r):
        bins, weights = bins_ref[r].astype(I32), int_ref[r].astype(F32)
        moved = bins + shift_ref[r, 0:1, :]
        hi_ref[:, 0:LANES] = (bins >> 6).astype(F32)
        hi_ref[:, LANES:] = (moved >> 6).astype(F32)
        lo_ref[:, 0:LANES] = (bins & (LOS - 1)).astype(F32)
        lo_ref[:, LANES:] = (moved & (LOS - 1)).astype(F32)
        w_ref[:, 0:LANES] = weights
        w_ref[:, LANES:] = weights
        hi_ids = iota((HIS, 2 * LANES), 0).astype(F32)
        lo_ids = iota((LOS, 2 * LANES), 0).astype(F32)
        left = iota((HIS, LANES), 1) < LOS

        def some(i, carry):
            at = pl.ds(pl.multiple_of(i * UNROLL, UNROLL), UNROLL)
            his, los, ws = hi_ref[at, :], lo_ref[at, :], w_ref[at, :]
            for c in range(0, UNROLL, 2):
                a = [jnp.where(hi_ids == his[e : e + 1, :], ws[e : e + 1, :], 0.0).astype(BF) for e in (c, c + 1)]
                b = [jnp.where(lo_ids == los[e : e + 1, :], 1.0, 0.0).astype(BF) for e in (c, c + 1)]
                d = lax.dot_general(
                    jnp.concatenate(a, 0), jnp.concatenate(b, 0), (((1,), (1,)), ((), ())),
                    preferred_element_type=F32,
                )
                row = pl.multiple_of(i * (UNROLL * 8), UNROLL * 8) + c * 8
                tall[pl.ds(row, HIS), :] = jnp.where(left, d[:HIS], d[HIS:])
            return carry

        lax.fori_loop(0, CB // UNROLL, some, 0)
        half = iota((CB // 2, LANES), 1) < LOS
        for j in range(CHUNKS):
            e = tall[pl.ds(2 * j, CB // 2, stride=HIS), :]
            f = tall[pl.ds(2 * j + 1, CB // 2, stride=HIS), :]
            at = slice(j * LANES, (j + 1) * LANES)
            dense[r, 0 : CB // 2, at] = jnp.where(half, e, pltpu.roll(f, LOS, 1)).astype(BF)
            dense[r, CB // 2 :, at] = jnp.where(half, pltpu.roll(e, LOS, 1), f).astype(BF)

    def to_mate(r):
        return pltpu.make_async_remote_copy(
            src_ref=dense.at[r], dst_ref=dense.at[3 + r], send_sem=mate_send.at[r], recv_sem=mate_recv.at[r],
            device_id=mate, device_id_type=MESH,
        )

    for load in loads[2:]:
        load.wait()
    bins_ref[0] = peaks_ref[...].astype(jnp.int16)
    shift_ref[0] = jnp.full((8, LANES), shift_smem[0], I32)
    densify(0)
    pl.semaphore_wait(barrier, NL - 1 + NX - 1 + core)

    raw = []
    for slot, to in ((1, lax.rem(l + 1, NL)), (2, lax.rem(l + NL - 1, NL))):
        for i, ref in enumerate((bins_ref, int_ref, shift_ref)):
            raw.append(
                pltpu.make_async_remote_copy(
                    src_ref=ref.at[0], dst_ref=ref.at[slot], send_sem=raw_send.at[slot - 1, i],
                    recv_sem=raw_recv.at[slot - 1, i], device_id=(to, q), device_id_type=MESH,
                )
            )
    for copy in raw:
        copy.start()

    def sent(b):
        return range(b * NL // 4, min((b + 1) * NL // 4, NL - 1))

    def deal(b):
        for i in sent(b):
            pltpu.make_async_remote_copy(
                src_ref=outgoing.at[i], dst_ref=qbuf.at[0, i], send_sem=a2a_send.at[b],
                recv_sem=a2a_recv.at[i // PSRC], device_id=ahead(i), device_id_type=MESH,
            ).start()

    def dealt(b):
        gone = outgoing.at[pl.ds(sent(b).start, len(sent(b)))]
        pltpu.make_async_copy(gone, gone, a2a_send.at[b]).wait()

    mates = [to_mate(r) for r in range(3)]

    def neighbour(slot):
        if slot:
            for i in range(3):
                raw[(slot - 1) * 3 + i].wait_recv()
            densify(slot)

        @pl.when(core == 1)
        def _():
            mates[slot].start()

    forwards = {}

    def forward(p):
        piece = pl.ds(p * PSRC, PSRC)
        arrived = qbuf.at[0, pl.ds(p * PSRC, PSRC - 1) if p == PIECES - 1 else piece]
        pltpu.make_async_copy(arrived, arrived, a2a_recv.at[p]).wait()
        copies = [
            pltpu.make_async_remote_copy(
                src_ref=qbuf.at[0, piece], dst_ref=qbuf.at[dx, piece], send_sem=fwd_send.at[p, dx - 1],
                recv_sem=fwd_recv.at[p, dx - 1], device_id=beside(dx), device_id_type=MESH,
            )
            for dx in range(1, NX)
        ]
        for copy in copies:
            copy.start()
        forwards[p] = copies

    def score(h):
        for p in range(h * PIECES // BATCHES, (h + 1) * PIECES // BATCHES):
            for copy in forwards[p]:
                copy.wait_recv()
        for dx in range(NX):
            part = qbuf[dx, pl.ds(h * BSRC, BSRC)].reshape(BSRC * 16, LANES)
            tall[pl.ds(dx * BSRC * 16, BSRC * 16), :] = part.astype(F32)
        for j in range(CHUNKS):
            for dx in range(NX):
                for s in range(2):
                    qmat[pl.ds((dx * 2 + s) * BSRC, BSRC), j * LANES : (j + 1) * LANES] = tall[
                        pl.ds(dx * BSRC * 16 + s * 8 + j, BSRC, stride=16), :
                    ].astype(BF)
        tops = []
        for b in range(6):
            if not scored and b == 3:

                @pl.when(core == 1)
                def _():
                    mates[0].wait_recv()

                for copy in mates[1:]:
                    copy.wait_recv()
            scores = lax.dot_general(
                dense[b], qmat[...], (((1,), (1,)), ((), ())), preferred_element_type=F32
            )
            tops.append(jnp.max(scores, axis=0, keepdims=True))
        return jnp.concatenate(tops + [jnp.zeros((2, NX * 2 * BSRC), F32)], axis=0)

    scored = []

    def give_back(b, maxima):
        turned = jnp.concatenate([maxima, jnp.zeros((LANES - 8, LANES), F32)], axis=0).T
        batch = pl.ds(b * BSRC, BSRC)
        for dx in range(NX):
            first = turned[dx * WIDTH : dx * WIDTH + BSRC]
            second = turned[dx * WIDTH + BSRC : (dx + 1) * WIDTH]
            ret_src[dx, batch, 0, :] = first + pltpu.roll(second, LANES // 2, 1)
        for i in range(b * BSRC, (b + 1) * BSRC):
            lib_of, _ = behind(i)
            for dx in (2, 1, 3, 0):
                if dx or i < NL - 1:
                    pltpu.make_async_remote_copy(
                        src_ref=ret_src.at[dx, i], dst_ref=ret_dst.at[dx, i], send_sem=ret_send.at[min(dx, 1)],
                        recv_sem=ret_recv.at[min(dx, 1)], device_id=(lib_of, beside(NX - dx)[1] if dx else q),
                        device_id_type=MESH,
                    ).start()
        scored.append(b)

    def answer_mate():
        @pl.when(core == 0)
        def _():
            mates[0].wait_recv()
            for copy in mates:
                copy.start()

    steps = {
        "a": deal,
        "w": dealt,
        "d": neighbour,
        "f": forward,
        "m": lambda _: answer_mate(),
        "s": lambda b: give_back(b, score(b)),
    }
    for step in SCHEDULE:
        steps[step[0]](int(step[1:] or 0))
    ret_dst[0, NL - 1] = ret_src[0, NL - 1]

    window = to_column(window_ref[...].astype(F32)).astype(I32)
    lanes = []
    for k in range(8):
        block_id = window + k
        r, col = block_id // 8, block_id % 8
        dx = (col // 2 - x + NX) % NX
        slot = jnp.where(r == 0, 1, jnp.where(r == 1, 0, 2))
        row = jnp.where(col % 2 == core, slot, 3 + slot)
        out_of_range = ((owner == 0) & (r == 0)) | ((owner == NL - 1) & (r == 2))
        target = dx * 8 + row + turn.astype(I32) * 64
        lanes.append(jnp.where(out_of_range, -1, target))
    take = jnp.where(iota((ROWS, NL), 1) == place.astype(I32), 1.0, 0.0)

    others = pl.ds(0, NL - 1)
    mine, theirs = ret_dst.at[0, others], ret_dst.at[pl.ds(1, NX - 1)]
    pltpu.make_async_copy(theirs, theirs, ret_recv.at[1]).wait()
    pltpu.make_async_copy(mine, mine, ret_recv.at[0]).wait()
    wide = ret_dst[0, :, 0, :]
    for dx in range(1, NX):
        wide = wide + pltpu.roll(ret_dst[dx, :, 0, :], dx * 8, 1)
    mine = jnp.dot(take, wide, precision=lax.Precision.HIGHEST, preferred_element_type=F32)
    result = jnp.zeros((ROWS, LANES), F32)
    for k in range(8):
        value = jnp.sum(jnp.where(iota((ROWS, LANES), 1) == lanes[k], mine, 0.0), axis=1, keepdims=True)
        result = jnp.where(iota((ROWS, LANES), 1) == k, value, result)
    out_ref[...] = result[:, 0:8]

    for copy in raw:
        copy.wait_send()
    for copy in mates:
        copy.wait_send()
    for copies in forwards.values():
        for copy in copies:
            copy.wait_send()
    for b in range(4):
        if f"w{b}" not in SCHEDULE:
            dealt(b)
    mine, theirs = ret_src.at[0, others], ret_src.at[pl.ds(1, NX - 1)]
    pltpu.make_async_copy(mine, mine, ret_send.at[0]).wait()
    pltpu.make_async_copy(theirs, theirs, ret_send.at[1]).wait()


def per_device(queries, owner, window_start, peak_bins, peak_int, block_shift):
    dma = pltpu.SemaphoreType.DMA
    hbm = pl.BlockSpec(memory_space=pltpu.HBM)
    return pl.pallas_call(
        kernel,
        out_shape=pltpu.VMEM((ROWS, 8), F32),
        in_specs=[hbm] * 5 + [pl.BlockSpec(memory_space=pltpu.SMEM)],
        out_specs=pl.BlockSpec(memory_space=pltpu.VMEM),
        scratch_shapes=[
            pltpu.VMEM((ROWS, B), BF),
            pltpu.VMEM((1, ROWS), I32),
            pltpu.VMEM((1, ROWS), I32),
            pltpu.VMEM((CB, LANES), I32),
            pltpu.VMEM((3, CB, LANES), jnp.int16),
            pltpu.VMEM((3, CB, LANES), BF),
            pltpu.VMEM((3, 8, LANES), I32),
            dma((5,)),
            pltpu.VMEM((2048, LANES), F32),
            pltpu.VMEM((NL, 16, LANES), BF),
            pltpu.VMEM((NX, NL, 16, LANES), BF),
            pltpu.VMEM((NX * 2 * BSRC, B), BF),
            pltpu.VMEM((CB, 2 * LANES), F32),
            pltpu.VMEM((CB, 2 * LANES), F32),
            pltpu.VMEM((CB, 2 * LANES), F32),
            pltpu.VMEM((6, CB, B), BF),
            pltpu.VMEM((NX, NL, 1, LANES), F32),
            pltpu.VMEM((NX, NL, 1, LANES), F32),
            dma((2, 3)), dma((2, 3)),
            dma((3,)), dma((3,)),
            dma((4,)), dma((PIECES,)),
            dma((PIECES, NX - 1)), dma((PIECES, NX - 1)),
            dma((2,)), dma((2,)),
        ],
        compiler_params=pltpu.CompilerParams(
            collective_id=0, has_side_effects=True, vmem_limit_bytes=60 * 1024 * 1024
        ),
    )(
        queries, owner.reshape(1, ROWS), window_start.reshape(1, ROWS), peak_bins, peak_int,
        block_shift,
    )


def solution(mesh):
    both = ("lib", "qry")
    placed = (P(both, None), P(both, None), P(both), P(both, None), P(both, None), P(both))
    return jax.shard_map(
        per_device, mesh=mesh, in_specs=placed, out_specs=P(both, None), check_vma=False
    )
```

```python
import jax
import jax.numpy as jnp
from jax import lax
from jax.experimental import pallas as pl
from jax.experimental.pallas import tpu as pltpu
from jax.sharding import PartitionSpec as P

MESH = pl.DeviceIdType.MESH
B = 1024
NZ, NY, NX = 16, 4, 4
NL = NZ * NY
ROWS = 64
CB = 128
LANES = 128
CHUNKS = B // LANES
BATCHES = 4
BSRC = NL // BATCHES
WIDTH = 2 * BSRC
PIECES = 8
PSRC = NL // PIECES
SCHEDULE = ("a0", "a1", "d0", "w0", "a2", "d1", "w1", "a3", "d2", "f0", "f1", "f2", "f3", "f4", "f5", "f6", "f7", "m", "s0", "s1", "s2", "s3")
DZS = (8, 7, 9, 6, 10, 5, 11, 4, 12, 3, 13, 2, 14, 1, 15, 0)
DYS = (2, 1, 3, 0)
OFFSETS = [(dz, dy) for dz in DZS for dy in DYS]
HIS, LOS = 16, 64
UNROLL = 32
BF, F32, I32 = jnp.bfloat16, jnp.float32, jnp.int32


def iota(shape, axis):
    return lax.broadcasted_iota(I32, shape, axis)


def place_of(owner, l):
    dz = (owner // NY - l // NY + NZ) % NZ
    dy = (owner % NY - l % NY + NY) % NY
    k = jnp.where(dz == 0, NZ - 1, jnp.where(dz < 8, 15 - 2 * dz, jnp.where(dz == 8, 0, 2 * dz - 16)))
    return k * NY + jnp.where(dy == 0, 3, jnp.where(dy == 3, 2, jnp.where(dy == 1, 1, 0)))


def to_row(column):
    n = column.shape[0]
    return jnp.sum(jnp.where(iota((n, n), 0) == iota((n, n), 1), column, 0.0), axis=0, keepdims=True)


def to_column(row):
    n = row.shape[1]
    return jnp.sum(jnp.where(iota((n, n), 0) == iota((n, n), 1), row, 0.0), axis=1, keepdims=True)


def kernel(
    q_hbm, owner_hbm, window_hbm, bins_hbm, int_hbm, shift_smem,
    out_ref,
    q_ref, owner_ref, window_ref, peaks_ref, bins_ref, int_ref, shift_ref, load_sem,
    tall, outgoing, qbuf, qmat, hi_ref, lo_ref, w_ref, dense, ret_src, ret_dst,
    raw_send, raw_recv, mate_send, mate_recv, a2a_send, a2a_recv, fwd_send, fwd_recv,
    ret_send, ret_recv,
):
    l, q = lax.axis_index("lib"), lax.axis_index("qry")
    x, core = q // 2, q % 2
    mate = (l, x * 2 + 1 - core)
    along_z = [lax.rem(l // NY + dz, NZ) * NY for dz in range(NZ)]
    along_y = [lax.rem(l % NY + dy, NY) for dy in range(NY)]

    def ahead(i):
        dz, dy = OFFSETS[i]
        return (along_z[dz] + along_y[dy], q)

    def behind(i):
        dz, dy = OFFSETS[i]
        return (along_z[-dz % NZ] + along_y[-dy % NY], q)

    def beside(dx):
        return (l, lax.rem(x + dx, NX) * 2 + core)

    loads = [
        pltpu.make_async_copy(src, dst, load_sem.at[i])
        for i, (src, dst) in enumerate(
            (
                (owner_hbm, owner_ref),
                (q_hbm, q_ref),
                (window_hbm, window_ref),
                (bins_hbm, peaks_ref),
                (int_hbm, int_ref.at[0]),
            )
        )
    ]
    for load in loads:
        load.start()

    barrier = pltpu.get_barrier_semaphore()

    for i in range(NL - 1):
        pl.semaphore_signal(barrier, inc=1, device_id=ahead(i), device_id_type=MESH)
    for dx in range(1, NX):
        pl.semaphore_signal(barrier, inc=1, device_id=beside(dx), device_id_type=MESH)

    @pl.when(core == 0)
    def _():
        pl.semaphore_signal(barrier, inc=1, device_id=mate, device_id_type=MESH)

    for load in loads[:2]:
        load.wait()

    owner_row = owner_ref[...].astype(F32)
    owner_col = to_column(owner_row)
    owner = owner_col.astype(I32)
    square = (ROWS, ROWS)
    earlier = (owner_col == owner_row) & (iota(square, 1) < iota(square, 0))
    turn = jnp.sum(jnp.where(earlier, 1.0, 0.0), axis=1, keepdims=True)
    place = place_of(owner, l).astype(F32)
    slot_row = to_row(place * 2.0 + turn)
    pick = jnp.where(iota((2 * NL, ROWS), 0).astype(F32) == slot_row, 1.0, 0.0).astype(BF)
    rows = jnp.dot(pick, q_ref[...], preferred_element_type=F32)
    for j in range(CHUNKS):
        tall[pl.ds(j, 2 * NL, stride=CHUNKS), :] = rows[:, j * LANES : (j + 1) * LANES]
    outgoing[...] = tall[0 : NL * 16, :].astype(BF).reshape(NL, 16, LANES)
    qbuf[0, NL - 1] = outgoing[NL - 1]

    def densify(r):
        bins, weights = bins_ref[r].astype(I32), int_ref[r].astype(F32)
        moved = bins + shift_ref[r, 0:1, :]
        hi_ref[:, 0:LANES] = (bins >> 6).astype(F32)
        hi_ref[:, LANES:] = (moved >> 6).astype(F32)
        lo_ref[:, 0:LANES] = (bins & (LOS - 1)).astype(F32)
        lo_ref[:, LANES:] = (moved & (LOS - 1)).astype(F32)
        w_ref[:, 0:LANES] = weights
        w_ref[:, LANES:] = weights
        hi_ids = iota((HIS, 2 * LANES), 0).astype(F32)
        lo_ids = iota((LOS, 2 * LANES), 0).astype(F32)
        left = iota((HIS, LANES), 1) < LOS

        def some(i, carry):
            at = pl.ds(pl.multiple_of(i * UNROLL, UNROLL), UNROLL)
            his, los, ws = hi_ref[at, :], lo_ref[at, :], w_ref[at, :]
            for c in range(0, UNROLL, 2):
                a = [jnp.where(hi_ids == his[e : e + 1, :], ws[e : e + 1, :], 0.0).astype(BF) for e in (c, c + 1)]
                b = [jnp.where(lo_ids == los[e : e + 1, :], 1.0, 0.0).astype(BF) for e in (c, c + 1)]
                d = lax.dot_general(
                    jnp.concatenate(a, 0), jnp.concatenate(b, 0), (((1,), (1,)), ((), ())),
                    preferred_element_type=F32,
                )
                row = pl.multiple_of(i * (UNROLL * 8), UNROLL * 8) + c * 8
                tall[pl.ds(row, HIS), :] = jnp.where(left, d[:HIS], d[HIS:])
            return carry

        lax.fori_loop(0, CB // UNROLL, some, 0)
        half = iota((CB // 2, LANES), 1) < LOS
        for j in range(CHUNKS):
            e = tall[pl.ds(2 * j, CB // 2, stride=HIS), :]
            f = tall[pl.ds(2 * j + 1, CB // 2, stride=HIS), :]
            at = slice(j * LANES, (j + 1) * LANES)
            dense[r, 0 : CB // 2, at] = jnp.where(half, e, pltpu.roll(f, LOS, 1)).astype(BF)
            dense[r, CB // 2 :, at] = jnp.where(half, pltpu.roll(e, LOS, 1), f).astype(BF)

    def to_mate(r):
        return pltpu.make_async_remote_copy(
            src_ref=dense.at[r], dst_ref=dense.at[3 + r], send_sem=mate_send.at[r], recv_sem=mate_recv.at[r],
            device_id=mate, device_id_type=MESH,
        )

    for load in loads[2:]:
        load.wait()
    bins_ref[0] = peaks_ref[...].astype(jnp.int16)
    shift_ref[0] = jnp.full((8, LANES), shift_smem[0], I32)
    densify(0)
    pl.semaphore_wait(barrier, NL - 1 + NX - 1 + core)

    raw = []
    for slot, to in ((1, lax.rem(l + 1, NL)), (2, lax.rem(l + NL - 1, NL))):
        for i, ref in enumerate((bins_ref, int_ref, shift_ref)):
            raw.append(
                pltpu.make_async_remote_copy(
                    src_ref=ref.at[0], dst_ref=ref.at[slot], send_sem=raw_send.at[slot - 1, i],
                    recv_sem=raw_recv.at[slot - 1, i], device_id=(to, q), device_id_type=MESH,
                )
            )
    for copy in raw:
        copy.start()

    def sent(b):
        return range(b * NL // 4, min((b + 1) * NL // 4, NL - 1))

    def deal(b):
        for i in sent(b):
            pltpu.make_async_remote_copy(
                src_ref=outgoing.at[i], dst_ref=qbuf.at[0, i], send_sem=a2a_send.at[b],
                recv_sem=a2a_recv.at[i // PSRC], device_id=ahead(i), device_id_type=MESH,
            ).start()

    def dealt(b):
        gone = outgoing.at[pl.ds(sent(b).start, len(sent(b)))]
        pltpu.make_async_copy(gone, gone, a2a_send.at[b]).wait()

    mates = [to_mate(r) for r in range(3)]

    def neighbour(slot):
        if slot:
            for i in range(3):
                raw[(slot - 1) * 3 + i].wait_recv()
            densify(slot)

        @pl.when(core == 1)
        def _():
            mates[slot].start()

    forwards = {}

    def forward(p):
        piece = pl.ds(p * PSRC, PSRC)
        arrived = qbuf.at[0, pl.ds(p * PSRC, PSRC - 1) if p == PIECES - 1 else piece]
        pltpu.make_async_copy(arrived, arrived, a2a_recv.at[p]).wait()
        copies = [
            pltpu.make_async_remote_copy(
                src_ref=qbuf.at[0, piece], dst_ref=qbuf.at[dx, piece], send_sem=fwd_send.at[p, dx - 1],
                recv_sem=fwd_recv.at[p, dx - 1], device_id=beside(dx), device_id_type=MESH,
            )
            for dx in range(1, NX)
        ]
        for copy in copies:
            copy.start()
        forwards[p] = copies

    def score(h):
        for p in range(h * PIECES // BATCHES, (h + 1) * PIECES // BATCHES):
            for copy in forwards[p]:
                copy.wait_recv()
        for dx in range(NX):
            part = qbuf[dx, pl.ds(h * BSRC, BSRC)].reshape(BSRC * 16, LANES)
            tall[pl.ds(dx * BSRC * 16, BSRC * 16), :] = part.astype(F32)
        for j in range(CHUNKS):
            for dx in range(NX):
                for s in range(2):
                    qmat[pl.ds((dx * 2 + s) * BSRC, BSRC), j * LANES : (j + 1) * LANES] = tall[
                        pl.ds(dx * BSRC * 16 + s * 8 + j, BSRC, stride=16), :
                    ].astype(BF)
        tops = []
        for b in range(6):
            if not scored and b == 3:

                @pl.when(core == 1)
                def _():
                    mates[0].wait_recv()

                for copy in mates[1:]:
                    copy.wait_recv()
            scores = lax.dot_general(
                dense[b], qmat[...], (((1,), (1,)), ((), ())), preferred_element_type=F32
            )
            tops.append(jnp.max(scores, axis=0, keepdims=True))
        return jnp.concatenate(tops + [jnp.zeros((2, NX * 2 * BSRC), F32)], axis=0)

    scored = []

    def give_back(b, maxima):
        turned = jnp.concatenate([maxima, jnp.zeros((LANES - 8, LANES), F32)], axis=0).T
        batch = pl.ds(b * BSRC, BSRC)
        for dx in range(NX):
            first = turned[dx * WIDTH : dx * WIDTH + BSRC]
            second = turned[dx * WIDTH + BSRC : (dx + 1) * WIDTH]
            ret_src[dx, batch, 0, :] = first + pltpu.roll(second, LANES // 2, 1)
        for i in range(b * BSRC, (b + 1) * BSRC):
            lib_of, _ = behind(i)
            for dx in (2, 1, 3, 0):
                if dx or i < NL - 1:
                    pltpu.make_async_remote_copy(
                        src_ref=ret_src.at[dx, i], dst_ref=ret_dst.at[dx, i], send_sem=ret_send.at[min(dx, 1)],
                        recv_sem=ret_recv.at[min(dx, 1)], device_id=(lib_of, beside(NX - dx)[1] if dx else q),
                        device_id_type=MESH,
                    ).start()
        scored.append(b)

    def answer_mate():
        @pl.when(core == 0)
        def _():
            mates[0].wait_recv()
            for copy in mates:
                copy.start()

    steps = {
        "a": deal,
        "w": dealt,
        "d": neighbour,
        "f": forward,
        "m": lambda _: answer_mate(),
        "s": lambda b: give_back(b, score(b)),
    }
    for step in SCHEDULE:
        steps[step[0]](int(step[1:] or 0))
    ret_dst[0, NL - 1] = ret_src[0, NL - 1]

    window = to_column(window_ref[...].astype(F32)).astype(I32)
    lanes = []
    for k in range(8):
        block_id = window + k
        r, col = block_id // 8, block_id % 8
        dx = (col // 2 - x + NX) % NX
        slot = jnp.where(r == 0, 1, jnp.where(r == 1, 0, 2))
        row = jnp.where(col % 2 == core, slot, 3 + slot)
        out_of_range = ((owner == 0) & (r == 0)) | ((owner == NL - 1) & (r == 2))
        target = dx * 8 + row + turn.astype(I32) * 64
        lanes.append(jnp.where(out_of_range, -1, target))
    take = jnp.where(iota((ROWS, NL), 1) == place.astype(I32), 1.0, 0.0)

    others = pl.ds(0, NL - 1)
    mine, theirs = ret_dst.at[0, others], ret_dst.at[pl.ds(1, NX - 1)]
    pltpu.make_async_copy(theirs, theirs, ret_recv.at[1]).wait()
    pltpu.make_async_copy(mine, mine, ret_recv.at[0]).wait()
    wide = ret_dst[0, :, 0, :]
    for dx in range(1, NX):
        wide = wide + pltpu.roll(ret_dst[dx, :, 0, :], dx * 8, 1)
    mine = jnp.dot(take, wide, precision=lax.Precision.HIGHEST, preferred_element_type=F32)
    result = jnp.zeros((ROWS, LANES), F32)
    for k in range(8):
        value = jnp.sum(jnp.where(iota((ROWS, LANES), 1) == lanes[k], mine, 0.0), axis=1, keepdims=True)
        result = jnp.where(iota((ROWS, LANES), 1) == k, value, result)
    out_ref[...] = result[:, 0:8]

    for copy in raw:
        copy.wait_send()
    for copy in mates:
        copy.wait_send()
    for copies in forwards.values():
        for copy in copies:
            copy.wait_send()
    for b in range(4):
        if f"w{b}" not in SCHEDULE:
            dealt(b)
    mine, theirs = ret_src.at[0, others], ret_src.at[pl.ds(1, NX - 1)]
    pltpu.make_async_copy(mine, mine, ret_send.at[0]).wait()
    pltpu.make_async_copy(theirs, theirs, ret_send.at[1]).wait()


def per_device(queries, owner, window_start, peak_bins, peak_int, block_shift):
    dma = pltpu.SemaphoreType.DMA
    hbm = pl.BlockSpec(memory_space=pltpu.HBM)
    return pl.pallas_call(
        kernel,
        out_shape=pltpu.VMEM((ROWS, 8), F32),
        in_specs=[hbm] * 5 + [pl.BlockSpec(memory_space=pltpu.SMEM)],
        out_specs=pl.BlockSpec(memory_space=pltpu.VMEM),
        scratch_shapes=[
            pltpu.VMEM((ROWS, B), BF),
            pltpu.VMEM((1, ROWS), I32),
            pltpu.VMEM((1, ROWS), I32),
            pltpu.VMEM((CB, LANES), I32),
            pltpu.VMEM((3, CB, LANES), jnp.int16),
            pltpu.VMEM((3, CB, LANES), BF),
            pltpu.VMEM((3, 8, LANES), I32),
            dma((5,)),
            pltpu.VMEM((2048, LANES), F32),
            pltpu.VMEM((NL, 16, LANES), BF),
            pltpu.VMEM((NX, NL, 16, LANES), BF),
            pltpu.VMEM((NX * 2 * BSRC, B), BF),
            pltpu.VMEM((CB, 2 * LANES), F32),
            pltpu.VMEM((CB, 2 * LANES), F32),
            pltpu.VMEM((CB, 2 * LANES), F32),
            pltpu.VMEM((6, CB, B), BF),
            pltpu.VMEM((NX, NL, 1, LANES), F32),
            pltpu.VMEM((NX, NL, 1, LANES), F32),
            dma((2, 3)), dma((2, 3)),
            dma((3,)), dma((3,)),
            dma((4,)), dma((PIECES,)),
            dma((PIECES, NX - 1)), dma((PIECES, NX - 1)),
            dma((2,)), dma((2,)),
        ],
        compiler_params=pltpu.CompilerParams(
            collective_id=0, has_side_effects=True, vmem_limit_bytes=60 * 1024 * 1024
        ),
    )(
        queries, owner.reshape(1, ROWS), window_start.reshape(1, ROWS), peak_bins, peak_int,
        block_shift,
    )


def solution(mesh):
    both = ("lib", "qry")
    placed = (P(both, None), P(both, None), P(both), P(both, None), P(both, None), P(both))
    return jax.shard_map(
        per_device, mesh=mesh, in_specs=placed, out_specs=P(both, None), check_vma=False
    )
```
